256 devices in a mesh: row: 16 (over z, x_hi), col: 16 (over x_lo, y, core).
Axes of the slice: x: 4 (x_hi: 2, x_lo: 2; x = x_hi * 2 + x_lo), y: 4, z: 8, core: 2. Of those that a mesh axis runs over, the one named last changes fastest.
Arguments:
- pair: bfloat16 [768, 768, 128], P('row', 'col'), may hold values from -1000 to 1000, as said below
- ln_gain: float32 [128], replicated, may hold values from 0.25 to 1.75
- w_proj: bfloat16 [128, 512], replicated, may hold values from -0.5 to 0.5
- w_gate: bfloat16 [128, 128], replicated, may hold values from -0.5 to 0.5
- out_gain: float32 [128], replicated, may hold values from 0.25 to 1.75
- w_out: bfloat16 [128, 128], replicated, may hold values from -0.5 to 0.5
Outputs:
- update: bfloat16 [768, 768, 128], P('row', 'col')
The draws below stay inside these ranges and needn't reach their ends.
Inputs may be any that keep to these rules, and one draw needn't show every extreme that they name: `pair`: finite values.
All inputs are finite; a program needn't handle non-finite values.
Results may differ from the reference program's by a relative error of at most 0.0078.
Values may be sent and summed in bfloat16 or wider, within the bound.
A program may use at most 128 MiB of HBM per device.

```python
import jax
import jax.numpy as jnp
from jax import lax

C = 128
H = 128
BLK = 48
N = 768


def draw_pair(key, part):
    key = jax.random.fold_in(key, 7)
    noise = jax.random.truncated_normal(key, -4.0, 4.0, (N, N, C), jnp.float32)
    return noise.astype(jnp.bfloat16)


def gaussian(key, dims, deviation, reach, dtype=jnp.bfloat16):
    entries = jax.random.normal(key, dims, jnp.float32) * deviation
    return jnp.minimum(jnp.maximum(entries, -reach), reach).astype(dtype)


def setup_inputs(seed: int = 0) -> dict:
    seeds = jax.random.split(jax.random.key(seed), 7)
    pair = draw_pair(jax.random.fold_in(seeds[6], 71), 0)
    ln_gain = jnp.clip(1.0 + 0.15 * jax.random.normal(seeds[1], (C,), jnp.float32), 0.25, 1.75)
    w_proj = gaussian(seeds[2], (C, 4 * H), C ** -0.5, 0.5)
    w_gate = gaussian(seeds[3], (C, C), C ** -0.5, 0.5)
    out_gain = jnp.clip(1.0 + 0.15 * jax.random.normal(seeds[4], (H,), jnp.float32), 0.25, 1.75)
    w_out = gaussian(seeds[5], (H, C), H ** -0.5, 0.5)
    return dict(pair=pair, ln_gain=ln_gain, w_proj=w_proj, w_gate=w_gate, out_gain=out_gain, w_out=w_out)


epsilon = 1e-05

def normalize(values, scales):
    average = lax.optimization_barrier(jnp.mean(values, axis=-1, keepdims=True))
    centred = values - average
    spread = lax.optimization_barrier(jnp.mean(centred * centred, axis=-1, keepdims=True))
    return centred * lax.rsqrt(spread + epsilon) * scales.astype(jnp.float32)

def reference(pair, ln_gain, w_proj, w_gate, out_gain, w_out):

    def project_block(block):
        flattened = block.reshape(-1, C).astype(jnp.float32)
        normed = normalize(flattened, ln_gain).astype(jnp.bfloat16)
        projected = jnp.dot(normed, w_proj, preferred_element_type=jnp.float32)
        left_side = (jax.nn.sigmoid(projected[:, :H]) * projected[:, H:2 * H]).astype(jnp.bfloat16)
        right_side = (jax.nn.sigmoid(projected[:, 2 * H:3 * H]) * projected[:, 3 * H:]).astype(jnp.bfloat16)
        gating = jax.nn.sigmoid(jnp.dot(normed, w_gate, preferred_element_type=jnp.float32))
        return (left_side, right_side, gating)
    blocks = pair.reshape(N // BLK, BLK, N, C)
    left_side, right_side, gating = lax.map(project_block, blocks)
    left_side = left_side.reshape(N, N, H)
    right_side = right_side.reshape(N, N, H)
    gating = gating.reshape(N, N, C)
    product = jnp.einsum('ikh,jkh->ijh', left_side.astype(jnp.float32), right_side.astype(jnp.float32))
    product_normed = normalize(product, out_gain).astype(jnp.bfloat16)
    projected_out = jnp.dot(product_normed.reshape(-1, H), w_out, preferred_element_type=jnp.float32)
    return (gating * projected_out.reshape(N, N, C)).astype(jnp.bfloat16)
```

```python
import jax
import jax.numpy as jnp
from jax import lax
from jax.sharding import PartitionSpec as P

epsilon = 1e-05


def normalize(values, scales):
    average = jnp.mean(values, axis=-1, keepdims=True)
    centred = values - average
    spread = jnp.mean(centred * centred, axis=-1, keepdims=True)
    return centred * lax.rsqrt(spread + epsilon) * scales


def per_device(pair, ln_gain, w_proj, w_gate, out_gain, w_out):
    row_count, col_count, channels = pair.shape
    hidden = w_out.shape[0]
    rows, cols = lax.axis_size("row"), lax.axis_size("col")
    half = row_count // 2
    flattened = pair.reshape(row_count * col_count, channels).astype(jnp.float32)
    normed = normalize(flattened, ln_gain).astype(jnp.bfloat16)
    projected = jnp.dot(normed, w_proj, preferred_element_type=jnp.float32)
    left = (jax.nn.sigmoid(projected[:, :hidden]) * projected[:, hidden : 2 * hidden]).astype(jnp.bfloat16)
    right = (jax.nn.sigmoid(projected[:, 2 * hidden : 3 * hidden]) * projected[:, 3 * hidden :]).astype(
        jnp.bfloat16
    )
    gating = jax.nn.sigmoid(jnp.dot(normed, w_gate, preferred_element_type=jnp.float32))
    both = jnp.concatenate([left, right], axis=1).reshape(2, half * col_count, 2, hidden)
    both = both.transpose(3, 0, 2, 1).reshape(rows * cols, 2 * half * col_count)
    both = lax.all_to_all(both, ("row", "col"), 0, 0, tiled=True)
    both = both.reshape(rows, cols, 2, half, col_count).transpose(2, 0, 3, 1, 4)
    both = both.reshape(2, rows * half, cols * col_count)
    groups = [[2 * g, 2 * g + 1] for g in range(cols // 2)]
    b_all = lax.all_gather(both[1], "col", axis_index_groups=groups)
    product = jnp.einsum("ik,pjk->ipj", both[0], b_all, preferred_element_type=jnp.float32).astype(jnp.bfloat16)
    product = product.reshape(rows, half, 2, rows, half).transpose(0, 3, 1, 2, 4)
    product = product.reshape(rows * cols, half * col_count)
    product = lax.all_to_all(product, ("row", "col"), 0, 0, tiled=True)
    product = product.reshape(hidden, 2, half * col_count).transpose(1, 2, 0)
    product = product.reshape(row_count * col_count, hidden).astype(jnp.float32)
    product_normed = normalize(product, out_gain).astype(jnp.bfloat16)
    projected_out = jnp.dot(product_normed, w_out, preferred_element_type=jnp.float32)
    update = (gating * projected_out).astype(jnp.bfloat16)
    return update.reshape(row_count, col_count, channels)


def solution(mesh):
    in_specs = (P("row", "col", None), P(), P(), P(), P(), P())
    out_specs = P("row", "col", None)
    return jax.shard_map(per_device, mesh=mesh, in_specs=in_specs, out_specs=out_specs, check_vma=False)
```

```python
import functools

import jax
import jax.numpy as jnp
from jax import lax
from jax.experimental import pallas as pl
from jax.experimental.pallas import tpu as pltpu
from jax.sharding import PartitionSpec as P

epsilon = 1e-05
MESH = pl.DeviceIdType.MESH
BLK = 48
PAD = 64
HALF = 64
LAYER = 32
RING = 8
K = 768


def kernel(
    pair, ln_gain, w_proj, w_gate, gain, w_out, out,
    normed, wide, stage, gating, b_msg, a_msg, b_in, a_in, a_all, b_all, p_msg, p_in,
    send_sem, in_sem, ring_send, ring_recv,
):
    r, c = lax.axis_index("row"), lax.axis_index("col")
    z, xh = r // 2, r % 2
    x, y, e = xh * 2 + c // 8, (c // 2) % 4, c % 2
    me = xh * 16 + c

    def peer(k):
        k = k + e * (LAYER - 2 * k)
        t = (11 * k) % LAYER
        px, py, pe = (x + t // 8) % 4, (y + (t // 2) % 4) % 4, (e + t % 2) % 2
        return px // 2, (px % 2) * 8 + py * 2 + pe

    right = ((z + 1) % RING * 2 + xh, c)
    left = ((z + RING - 1) % RING * 2 + xh, c)

    barrier = pltpu.get_barrier_semaphore()

    @pl.loop(1, LAYER)
    def _(k):
        ph, pc = peer(k)
        pl.semaphore_signal(barrier, inc=1, device_id=(2 * z + ph, pc), device_id_type=MESH)

    pl.semaphore_signal(barrier, inc=1, device_id=right, device_id_type=MESH)
    pl.semaphore_signal(barrier, inc=1, device_id=left, device_id_type=MESH)

    wide[...] = jnp.zeros_like(wide)
    b_all[:, :, :, BLK:, :] = jnp.zeros((RING, 4, 2, PAD - BLK, K), jnp.bfloat16)

    @pl.loop(0, 6)
    def _(n):
        rows = pl.ds(n * 8, 8)
        values = pair[rows].astype(jnp.float32)
        average = jnp.mean(values, axis=-1, keepdims=True)
        centred = values - average
        spread = jnp.mean(centred * centred, axis=-1, keepdims=True)
        result = (centred * lax.rsqrt(spread + epsilon) * ln_gain[...].reshape(1, 1, 128)).astype(jnp.bfloat16)
        normed[rows] = result
        wide[rows, :BLK, :128] = result
        wide[rows, PAD : PAD + BLK, 128:] = result

    def project(which, msg):
        @pl.loop(0, 6)
        def _(n):
            block = wide[pl.ds(n * 8, 8)].reshape(8 * 128, 256)
            both = lax.dot_general(
                w_proj[which], block, (((1,), (1,)), ((), ())), preferred_element_type=jnp.float32
            )
            side = jax.nn.sigmoid(both[:HALF]) * both[HALF:]
            for j in range(8):
                stage[pl.ds(n * 8 + j, HALF, stride=BLK), :] = side[:, j * 128 : (j + 1) * 128]

        @pl.loop(0, LAYER)
        def _(n):
            msg[n] = stage[pl.ds(n * 96, 96), :].astype(jnp.bfloat16)

    def scatter(msg, into, i):
        @pl.loop(1, LAYER)
        def _(k):
            ph, pc = peer(k)
            pltpu.make_async_remote_copy(
                src_ref=msg.at[ph * 16 + pc], dst_ref=into.at[me],
                send_sem=send_sem.at[i], recv_sem=in_sem.at[i],
                device_id=(2 * z + ph, pc), device_id_type=MESH,
            ).start()

        pltpu.make_async_copy(msg.at[me], into.at[me], in_sem.at[i]).start()

    def arrived(into, i):
        pltpu.make_async_copy(into, into, in_sem.at[i]).wait()

    project(1, b_msg)
    pl.semaphore_wait(barrier, LAYER + 1)
    scatter(b_msg, b_in, 0)
    project(0, a_msg)
    scatter(a_msg, a_in, 1)

    def gathered(into, h, ch):
        rows, lanes = slice(ch // 2 * BLK, ch // 2 * BLK + BLK), slice(ch % 2 * PAD, ch % 2 * PAD + BLK)
        return jnp.concatenate([into[h * 16 + s, rows, lanes] for s in range(16)], axis=1)

    def ring_copy(step, ch, way):
        slot = step if way == 0 else (RING - step) % RING
        to = step + 1 if way == 0 else RING - 1 - step
        return pltpu.make_async_remote_copy(
            src_ref=b_all.at[slot, ch, :, pl.ds(0, BLK)], dst_ref=b_all.at[to, ch, :, pl.ds(0, BLK)],
            send_sem=ring_send.at[way, step, ch], recv_sem=ring_recv.at[way, step, ch],
            device_id=(right, left)[way], device_id_type=MESH,
        )

    arrived(b_in, 0)
    for ch, way in ((0, 0), (2, 1), (1, 0), (3, 1)):
        for h in range(2):
            b_all[0, ch, h, :BLK, :] = gathered(b_in, h, ch)
        ring_copy(0, ch, way).start()
    for ch, way in ((2, 0), (0, 1), (3, 0), (1, 1)):
        ring_copy(0, ch, way).start()

    @pl.loop(0, 6)
    def _(n):
        rows = pl.ds(n * 8, 8)
        gate = jnp.dot(normed[rows].reshape(8 * BLK, 128), w_gate[...], preferred_element_type=jnp.float32)
        gating[rows] = jax.nn.sigmoid(gate).reshape(8, BLK, 128)

    arrived(a_in, 1)
    for ch in range(4):
        for h in range(2):
            a_all[ch, h * BLK : (h + 1) * BLK, :] = gathered(a_in, h, ch)

    low = lax.broadcasted_iota(jnp.int32, (96, 128), 1) < PAD

    def multiply(slot, pp):
        one, two = [
            lax.dot_general(
                a_all[2 * pp + i], b_all[slot, 2 * pp + i].reshape(2 * PAD, K),
                (((1,), (1,)), ((), ())), preferred_element_type=jnp.float32,
            )
            for i in range(2)
        ]
        first = jnp.where(low, one, pltpu.roll(two, PAD, 1)).astype(jnp.bfloat16)
        second = jnp.where(low, pltpu.roll(one, PAD, 1), two).astype(jnp.bfloat16)
        zb = (z + RING - slot) % RING
        for je, value in ((0, first), (1, second)):
            for ih in range(2):
                p_msg[slot, pp, je, ih] = value[ih * BLK : (ih + 1) * BLK]
                src = p_msg.at[slot, pp, je, ih]
                dst = p_in.at[me * 2 + pp]
                here = jnp.logical_and(ih == xh, 2 * zb + je == c)

                @pl.when(here)
                def _():
                    pltpu.make_async_copy(src, dst, in_sem.at[2]).start()

                @pl.when(jnp.logical_not(here))
                def _():
                    pltpu.make_async_remote_copy(
                        src_ref=src, dst_ref=dst, send_sem=send_sem.at[2], recv_sem=in_sem.at[2],
                        device_id=(2 * z + ih, 2 * zb + je), device_id_type=MESH,
                    ).start()

    for pp in range(2):
        multiply(0, pp)

    @pl.loop(1, 4)
    def _(step):
        for pp in range(2):
            for way in range(2):
                pair_no = pp if way == 0 else 1 - pp
                for i in range(2):
                    ch = 2 * pair_no + i
                    ring_copy(step - 1, ch, way).wait_recv()
                    if pp == 0:
                        ring_copy(step, ch, way).start()
                    else:
                        @pl.when(step < 3)
                        def _():
                            ring_copy(step, ch, way).start()

                multiply(step if way == 0 else RING - step, pair_no)

    for way in range(2):
        for i in range(2):
            ring_copy(3, 2 * way + i, way).wait_recv()
        multiply(4, way)

    for i, msg in ((0, b_msg), (1, a_msg)):
        sent = msg.at[pl.ds(0, LAYER - 1)]
        pltpu.make_async_copy(sent, sent, send_sem.at[i]).wait()
    for way in range(2):
        for step in range(4):
            for ch in range(4):
                if step < 3 or ch // 2 == way:
                    ring_copy(step, ch, way).wait_send()

    sent = p_in.at[pl.ds(0, 2 * (LAYER - 1))]
    pltpu.make_async_copy(sent, sent, send_sem.at[2]).wait()
    arrived(p_in, 2)

    @pl.loop(0, 3)
    def _(n):
        rows = pl.ds(n * 16, 16)
        total = jnp.sum(p_in[:, rows, :].astype(jnp.float32), axis=0)
        average = (total + pltpu.roll(total, PAD, 1)) * (1.0 / 128)
        total = jnp.zeros((16, 128), jnp.float32)
        for s in range(HALF):
            centred = p_in[s, rows, :].astype(jnp.float32) - average
            total = total + centred * centred
        spread = (total + pltpu.roll(total, PAD, 1)) * (1.0 / 128)
        factor = lax.rsqrt(spread + epsilon)
        for s in range(HALF):
            centred = p_in[s, rows, :].astype(jnp.float32) - average
            stage[pl.ds(n * 16 + s * BLK, 16), :] = centred * factor * gain[s : s + 1, :]

    under = lax.broadcasted_iota(jnp.int32, (HALF, 128), 1) < PAD

    @pl.loop(0, BLK // 2)
    def _(n):
        one = stage[pl.ds(2 * n, HALF, stride=BLK), :]
        two = stage[pl.ds(2 * n + 1, HALF, stride=BLK), :]
        even = jnp.where(under, one, pltpu.roll(two, PAD, 1))
        odd = jnp.where(under, pltpu.roll(one, PAD, 1), two)
        both = jnp.concatenate([even, odd], axis=0).astype(jnp.bfloat16)
        result = lax.dot_general(both, w_out[...], (((0,), (0,)), ((), ())), preferred_element_type=jnp.float32)
        out[2 * n] = (gating[2 * n] * result[:BLK]).astype(jnp.bfloat16)
        out[2 * n + 1] = (gating[2 * n + 1] * result[PAD : PAD + BLK]).astype(jnp.bfloat16)


def per_device(pair, ln_gain, w_proj, w_gate, out_gain, w_out):
    bf16, f32 = jnp.bfloat16, jnp.float32
    w_wide = w_proj.reshape(128, 4, HALF, 2).transpose(1, 2, 3, 0).reshape(2, 128, 256)
    w_fold = w_out.reshape(HALF, 2, 128).transpose(1, 0, 2).reshape(128, 128)
    gain = jnp.repeat(out_gain.reshape(HALF, 2), PAD, axis=1)
    vmem = pl.BlockSpec(memory_space=pltpu.VMEM)
    dma = pltpu.SemaphoreType.DMA
    return pl.pallas_call(
        kernel,
        out_shape=jax.ShapeDtypeStruct(pair.shape, bf16),
        in_specs=[vmem] * 6,
        out_specs=vmem,
        scratch_shapes=[
            pltpu.VMEM((BLK, BLK, 128), bf16),
            pltpu.VMEM((BLK, 128, 256), bf16),
            pltpu.VMEM((HALF * BLK, 128), f32),
            pltpu.VMEM((BLK, BLK, 128), f32),
            pltpu.VMEM((LAYER, 96, 128), bf16),
            pltpu.VMEM((LAYER, 96, 128), bf16),
            pltpu.VMEM((LAYER, 96, 128), bf16),
            pltpu.VMEM((LAYER, 96, 128), bf16),
            pltpu.VMEM((4, 96, K), bf16),
            pltpu.VMEM((RING, 4, 2, PAD, K), bf16),
            pltpu.VMEM((RING, 2, 2, 2, BLK, 128), bf16),
            pltpu.VMEM((2 * LAYER, BLK, 128), bf16),
            dma((3,)), dma((3,)), dma((2, 4, 4)), dma((2, 4, 4)),
        ],
        compiler_params=pltpu.CompilerParams(
            collective_id=0, has_side_effects=True, vmem_limit_bytes=48 * 2**20
        ),
        name="triangle",
    )(pair, ln_gain.reshape(1, 128), w_wide, w_gate, gain, w_fold)


def solution(mesh):
    in_specs = (P("row", "col", None), P(), P(), P(), P(), P())
    out_specs = P("row", "col", None)
    return jax.shard_map(per_device, mesh=mesh, in_specs=in_specs, out_specs=out_specs, check_vma=False)
```

```python
import jax
import jax.numpy as jnp
from jax import lax
from jax.experimental import pallas as pl
from jax.experimental.pallas import tpu as pltpu
from jax.sharding import PartitionSpec as P

epsilon = 1e-05
MESH = pl.DeviceIdType.MESH
BLK = 48
PAD = 64
HALF = 64
LAYER = 32
RING = 8
K = 768
SUB = 16
PARTS = BLK // SUB
WINDOW = 2
LATE = 2


def kernel(
    pair_hbm, ln_gain_hbm, w_proj_hbm, w_gate_hbm, out_gain_hbm, w_out_hbm, out, ring,
    pair, ln_gain, w_proj, w_gate, out_gain, w_out, normed, wide, stage, gating, w_wide, w_fold, gain,
    b_msg, a_msg, b_in, a_in, a_all, b_all, p_msg, p_in,
    load_sem, small_sem, fetch_sem, b_send, b_recv, a_send, a_recv, p_send, p_recv, ring_send, ring_recv,
):
    r, c = lax.axis_index("row"), lax.axis_index("col")
    z, xh = r // 2, r % 2
    x, y, e = xh * 2 + c // 8, (c // 2) % 4, c % 2
    me = xh * 16 + c

    def load(part):
        rows = pl.ds(part * SUB, SUB)
        return pltpu.make_async_copy(pair_hbm.at[rows], pair.at[rows], load_sem.at[part])

    smalls = [
        pltpu.make_async_copy(src, dst, small_sem.at[i])
        for i, (src, dst) in enumerate((
            (w_proj_hbm, w_proj), (ln_gain_hbm, ln_gain), (w_gate_hbm, w_gate),
            (out_gain_hbm, out_gain), (w_out_hbm, w_out),
        ))
    ]
    smalls[0].start()
    for part in range(PARTS):
        load(part).start()
    for copy in smalls[1:]:
        copy.start()

    def peer(k):
        k = k + e * (LAYER - 2 * k)
        t = (11 * k) % LAYER
        px, py, pe = (x + t // 8) % 4, (y + (t // 2) % 4) % 4, (e + t % 2) % 2
        return px // 2, (px % 2) * 8 + py * 2 + pe

    beside = (((z + 1) % RING * 2 + xh, c), ((z + RING - 1) % RING * 2 + xh, c))

    barrier = pltpu.get_barrier_semaphore()

    @pl.loop(1, LAYER)
    def _(k):
        ph, pc = peer(k)
        pl.semaphore_signal(barrier, inc=1, device_id=(2 * z + ph, pc), device_id_type=MESH)

    for way in range(2):
        pl.semaphore_signal(barrier, inc=1, device_id=beside[way], device_id_type=MESH)

    wide[:, :, 128:] = jnp.zeros((BLK, 128, 128), jnp.bfloat16)
    wide[:, PAD:, :128] = jnp.zeros((BLK, PAD, 128), jnp.bfloat16)
    wide[:, BLK:PAD, :128] = jnp.zeros((BLK, PAD - BLK, 128), jnp.bfloat16)
    for copy in smalls:
        copy.wait()

    row = lax.broadcasted_iota(jnp.int32, (128, 128), 0)
    col = lax.broadcasted_iota(jnp.int32, (128, 128), 1)
    order = (col == row % HALF * 2 + row // HALF).astype(jnp.bfloat16)
    for t in range(4):
        turned = lax.dot_general(
            order, w_proj[:, t * 128 : (t + 1) * 128], (((1,), (1,)), ((), ())), preferred_element_type=jnp.float32
        ).astype(jnp.bfloat16)
        w_wide[t // 2, t % 2 * HALF : (t % 2 + 1) * HALF, :128] = turned[:HALF]
        w_wide[t // 2, t % 2 * HALF : (t % 2 + 1) * HALF, 128:] = turned[HALF:]

    def project(which, msg, part):
        block = wide[pl.ds(part * SUB, SUB)].reshape(SUB * 128, 256)
        both = lax.dot_general(
            w_wide[which], block, (((1,), (1,)), ((), ())), preferred_element_type=jnp.float32
        )
        side = jax.nn.sigmoid(both[:HALF]) * both[HALF:]
        for j in range(SUB):
            stage[pl.ds(j, HALF, stride=SUB), :] = side[:, j * 128 : (j + 1) * 128]
        msg[part] = stage[pl.ds(0, HALF * SUB)].reshape(LAYER, 2 * SUB, 128).astype(jnp.bfloat16)

    def scatter(msg, into, send, recv, part):
        @pl.loop(1, LAYER)
        def _(k):
            ph, pc = peer(k)
            pltpu.make_async_remote_copy(
                src_ref=msg.at[part, ph * 16 + pc], dst_ref=into.at[part, me], send_sem=send, recv_sem=recv,
                device_id=(2 * z + ph, pc), device_id_type=MESH,
            ).start()

        pltpu.make_async_copy(msg.at[part, me], into.at[part, me], recv).start()

    def whole(ref, sem):
        pltpu.make_async_copy(ref, ref, sem).wait()

    for part in range(PARTS):
        load(part).wait()
        rows = pl.ds(part * SUB, SUB)
        values = pair[rows].astype(jnp.float32)
        average = jnp.mean(values, axis=-1, keepdims=True)
        centred = values - average
        spread = jnp.mean(centred * centred, axis=-1, keepdims=True)
        result = (centred * lax.rsqrt(spread + epsilon) * ln_gain[...].reshape(1, 1, 128)).astype(jnp.bfloat16)
        normed[rows] = result
        wide[rows, :BLK, :128] = result
        wide[rows, PAD : PAD + BLK, 128:] = result
        project(1, b_msg, part)
        if part == 0:
            pl.semaphore_wait(barrier, LAYER + 1)
        scatter(b_msg, b_in, b_send.at[part], b_recv.at[part], part)

    def gathered(into, part, h, ch):
        rows, lanes = slice(ch // 2 * SUB, (ch // 2 + 1) * SUB), slice(ch % 2 * PAD, ch % 2 * PAD + BLK)
        return jnp.concatenate([into[part, h * 16 + s, rows, lanes] for s in range(16)], axis=1)

    def part_of(way, part):
        return pl.ds(2 * way, 2), slice(None), pl.ds(part * SUB, SUB)

    def ring_copy(step, part, way):
        block = part_of(way, part)
        src = b_all if isinstance(step, int) and step == 0 else ring
        return pltpu.make_async_remote_copy(
            src_ref=src.at[(step, *block)], dst_ref=ring.at[(step + 1, *block)],
            send_sem=ring_send.at[way, step, part], recv_sem=ring_recv.at[way, step, part],
            device_id=beside[way], device_id_type=MESH,
        )

    def fetch(step, part, way):
        block = part_of(way, part)
        return pltpu.make_async_copy(
            ring.at[(step, *block)], b_all.at[(step, *block)], fetch_sem.at[way, step, part]
        )

    for part in range(PARTS):
        project(0, a_msg, part)

    b_all[:, :, :, BLK:, :] = jnp.zeros((RING, 4, 2, PAD - BLK, K), jnp.bfloat16)
    for part in range(PARTS):
        whole(b_in.at[part], b_recv.at[part])
        for way in range(2):
            for h in range(2):
                for ch in (2 * way, 2 * way + 1):
                    b_all[0, ch, h, part * SUB : (part + 1) * SUB, :] = gathered(b_in, part, h, ch)
            if part >= WINDOW:
                ring_copy(0, part - WINDOW, way).wait_send()
            ring_copy(0, part, way).start()

    scatter(a_msg, a_in, a_send, a_recv, slice(None))

    @pl.loop(0, PARTS)
    def _(part):
        rows = pl.ds(part * SUB, SUB)
        gate = jnp.dot(normed[rows].reshape(SUB * BLK, 128), w_gate[...], preferred_element_type=jnp.float32)
        gating[rows] = jax.nn.sigmoid(gate).reshape(SUB, BLK, 128)

    def forward(step):
        for part in range(PARTS):
            for way in range(2):
                ring_copy(step - 1, part, way).wait_recv()
                if part >= WINDOW:
                    ring_copy(step, part - WINDOW, way).wait_send()
                else:
                    ring_copy(step - 1, part - WINDOW + PARTS, way).wait_send()
                ring_copy(step, part, way).start()
                fetch(step, part, way).start()

    low = lax.broadcasted_iota(jnp.int32, (2 * BLK, 128), 1) < PAD

    def multiply(step, way):
        if not (isinstance(step, int) and step == 0):
            for part in range(PARTS):
                fetch(step, part, way).wait()
        one, two = [
            lax.dot_general(
                a_all[2 * way + i], b_all[step, 2 * way + i].reshape(2 * PAD, K),
                (((1,), (1,)), ((), ())), preferred_element_type=jnp.float32,
            )
            for i in range(2)
        ]
        first = jnp.where(low, one, pltpu.roll(two, PAD, 1)).astype(jnp.bfloat16)
        second = jnp.where(low, pltpu.roll(one, PAD, 1), two).astype(jnp.bfloat16)
        zb = (z + RING - step if way == 0 else z + step) % RING
        for je, value in ((0, first), (1, second)):
            for ih in range(2):
                p_msg[step, way, je, ih] = value[ih * BLK : (ih + 1) * BLK]
                src = p_msg.at[step, way, je, ih]
                dst = p_in.at[me * 2 + way]
                here = jnp.logical_and(ih == xh, 2 * zb + je == c)

                @pl.when(here)
                def _():
                    pltpu.make_async_copy(src, dst, p_recv).start()

                @pl.when(jnp.logical_not(here))
                def _():
                    pltpu.make_async_remote_copy(
                        src_ref=src, dst_ref=dst, send_sem=p_send, recv_sem=p_recv,
                        device_id=(2 * z + ih, 2 * zb + je), device_id_type=MESH,
                    ).start()

    for step in range(1, LATE + 1):
        forward(step)

    whole(a_in, a_recv)
    for part in range(PARTS):
        for ch in range(4):
            for h in range(2):
                a_all[ch, h * BLK + part * SUB : h * BLK + (part + 1) * SUB, :] = gathered(a_in, part, h, ch)

    for way in range(2):
        multiply(0, way)

    @pl.loop(1, LATE + 1)
    def _(step):
        for way in range(2):
            multiply(step, way)

    @pl.loop(LATE + 1, RING - 1)
    def _(step):
        forward(step)
        for way in range(2):
            multiply(step, way)

    for way in range(2):
        for part in range(PARTS):
            ring_copy(RING - 2, part, way).wait_recv()
            fetch(RING - 1, part, way).start()
    for way in range(2):
        multiply(RING - 1, way)

    for part in range(PARTS):
        whole(b_msg.at[part, pl.ds(0, LAYER - 1)], b_send.at[part])
    whole(a_msg.at[:, pl.ds(0, LAYER - 1)], a_send)
    for way in range(2):
        for part in range(PARTS - WINDOW, PARTS):
            ring_copy(RING - 2, part, way).wait_send()
    whole(p_in.at[pl.ds(0, 2 * (LAYER - 1))], p_send)
    whole(p_in, p_recv)

    folded = lax.dot_general(order, w_out[...], (((1,), (0,)), ((), ())), preferred_element_type=jnp.float32)
    w_fold[...] = folded.astype(jnp.bfloat16)
    pairs = lax.broadcasted_iota(jnp.int32, (HALF, 128), 0)
    lanes = lax.broadcasted_iota(jnp.int32, (HALF, 128), 1)
    under = lanes < PAD
    picked = [
        jnp.sum(jnp.where(lanes == 2 * pairs + i, out_gain[...], 0.0), axis=1, keepdims=True) for i in range(2)
    ]
    gain[...] = jnp.where(under, picked[0], picked[1])

    @pl.loop(0, PARTS)
    def _(part):
        rows = pl.ds(part * SUB, SUB)
        total = jnp.sum(p_in[:, rows, :].astype(jnp.float32), axis=0)
        average = (total + pltpu.roll(total, PAD, 1)) * (1.0 / 128)
        total = jnp.zeros((SUB, 128), jnp.float32)
        for s in range(HALF):
            centred = p_in[s, rows, :].astype(jnp.float32) - average
            total = total + centred * centred
        spread = (total + pltpu.roll(total, PAD, 1)) * (1.0 / 128)
        factor = lax.rsqrt(spread + epsilon)
        for s in range(HALF):
            centred = p_in[s, rows, :].astype(jnp.float32) - average
            stage[pl.ds(part * SUB + s * BLK, SUB), :] = centred * factor * gain[s : s + 1, :]

    @pl.loop(0, 6)
    def _(n):
        blocks = []
        for i in range(4):
            one = stage[pl.ds(8 * n + 2 * i, HALF, stride=BLK), :]
            two = stage[pl.ds(8 * n + 2 * i + 1, HALF, stride=BLK), :]
            even = jnp.where(under, one, pltpu.roll(two, PAD, 1))
            odd = jnp.where(under, pltpu.roll(one, PAD, 1), two)
            blocks.append(jnp.concatenate([even, odd], axis=0).astype(jnp.bfloat16))
        both = jnp.concatenate(blocks, axis=1)
        result = lax.dot_general(both, w_fold[...], (((0,), (0,)), ((), ())), preferred_element_type=jnp.float32)
        for i in range(8):
            out[8 * n + i] = (gating[8 * n + i] * result[i * PAD : i * PAD + BLK]).astype(jnp.bfloat16)


def per_device(pair, ln_gain, w_proj, w_gate, out_gain, w_out):
    bf16, f32 = jnp.bfloat16, jnp.float32
    vmem = pl.BlockSpec(memory_space=pltpu.VMEM)
    dma = pltpu.SemaphoreType.DMA
    parts = (PARTS, LAYER, 2 * SUB, 128)
    update, _ = pl.pallas_call(
        kernel,
        out_shape=(
            jax.ShapeDtypeStruct(pair.shape, bf16),
            jax.ShapeDtypeStruct((RING, 4, 2, BLK, K), bf16),
        ),
        in_specs=[pl.BlockSpec(memory_space=pl.ANY)] * 6,
        out_specs=(vmem, pl.BlockSpec(memory_space=pl.ANY)),
        scratch_shapes=[
            pltpu.VMEM((BLK, BLK, 128), bf16),
            pltpu.VMEM((1, 128), f32),
            pltpu.VMEM((128, 512), bf16),
            pltpu.VMEM((128, 128), bf16),
            pltpu.VMEM((1, 128), f32),
            pltpu.VMEM((128, 128), bf16),
            pltpu.VMEM((BLK, BLK, 128), bf16),
            pltpu.VMEM((BLK, 128, 256), bf16),
            pltpu.VMEM((HALF * BLK, 128), f32),
            pltpu.VMEM((BLK, BLK, 128), f32),
            pltpu.VMEM((2, 128, 256), bf16),
            pltpu.VMEM((128, 128), bf16),
            pltpu.VMEM((HALF, 128), f32),
            pltpu.VMEM(parts, bf16),
            pltpu.VMEM(parts, bf16),
            pltpu.VMEM(parts, bf16),
            pltpu.VMEM(parts, bf16),
            pltpu.VMEM((4, 2 * BLK, K), bf16),
            pltpu.VMEM((RING, 4, 2, PAD, K), bf16),
            pltpu.VMEM((RING, 2, 2, 2, BLK, 128), bf16),
            pltpu.VMEM((2 * LAYER, BLK, 128), bf16),
            dma((PARTS,)), dma((5,)), dma((2, RING, PARTS)),
            dma((PARTS,)), dma((PARTS,)), dma, dma,
            dma, dma,
            dma((2, RING - 1, PARTS)), dma((2, RING - 1, PARTS)),
        ],
        compiler_params=pltpu.CompilerParams(
            collective_id=0, has_side_effects=True, vmem_limit_bytes=56 * 2**20
        ),
        name="triangle",
    )(pair, ln_gain.reshape(1, 128), w_proj, w_gate, out_gain.reshape(1, 128), w_out)
    return update


def solution(mesh):
    in_specs = (P("row", "col", None), P(), P(), P(), P(), P())
    out_specs = P("row", "col", None)
    return jax.shard_map(per_device, mesh=mesh, in_specs=in_specs, out_specs=out_specs, check_vma=False)
```

```python
import jax
import jax.numpy as jnp
from jax import lax
from jax.experimental import pallas as pl
from jax.experimental.pallas import tpu as pltpu
from jax.sharding import PartitionSpec as P

epsilon = 1e-05
MESH = pl.DeviceIdType.MESH
BLK = 48
PAD = 64
HALF = 64
LAYER = 32
RING = 8
K = 768
SUB = 16
PARTS = BLK // SUB
RAW = PARTS - 1


def kernel(
    pair_hbm, ln_gain_hbm, w_proj_hbm, w_gate_hbm, out_gain_hbm, w_out_hbm, out,
    pair, ln_gain, w_proj, w_gate, out_gain, w_out, normed, wide, stage, gating, w_wide, w_fold, gain,
    b_msg, a_msg, b_in, a_in, raw_in, raw_all, a_all, b_all, p_msg, p_in,
    load_sem, small_sem, b_send, b_recv, a_send, a_recv, raw_send, raw_recv, rest_send, rest_recv, p_send, p_recv, ring_send, ring_recv,
):
    r, c = lax.axis_index("row"), lax.axis_index("col")
    z, xh = r // 2, r % 2
    x, y, e = xh * 2 + c // 8, (c // 2) % 4, c % 2
    me = xh * 16 + c

    def load(part):
        rows = pl.ds(part * SUB, SUB)
        return pltpu.make_async_copy(pair_hbm.at[rows], pair.at[rows], load_sem.at[part])

    smalls = [
        pltpu.make_async_copy(src, dst, small_sem.at[i])
        for i, (src, dst) in enumerate((
            (w_proj_hbm, w_proj), (ln_gain_hbm, ln_gain), (w_gate_hbm, w_gate),
            (out_gain_hbm, out_gain), (w_out_hbm, w_out),
        ))
    ]
    smalls[0].start()
    for part in range(PARTS):
        load(part).start()
    for copy in smalls[1:]:
        copy.start()

    def peer(k):
        k = k + e * (LAYER - 2 * k)
        t = (11 * k) % LAYER
        px, py, pe = (x + t // 8) % 4, (y + (t // 2) % 4) % 4, (e + t % 2) % 2
        return px // 2, (px % 2) * 8 + py * 2 + pe

    beside = (((z + 1) % RING * 2 + xh, c), ((z + RING - 1) % RING * 2 + xh, c))

    barrier = pltpu.get_barrier_semaphore()

    @pl.loop(1, LAYER)
    def _(k):
        ph, pc = peer(k)
        pl.semaphore_signal(barrier, inc=1, device_id=(2 * z + ph, pc), device_id_type=MESH)

    for way in range(2):
        pl.semaphore_signal(barrier, inc=1, device_id=beside[way], device_id_type=MESH)

    wide[:, :, 128:] = jnp.zeros((BLK, 128, 128), jnp.bfloat16)
    wide[:, PAD:, :128] = jnp.zeros((BLK, PAD, 128), jnp.bfloat16)
    wide[:, BLK:PAD, :128] = jnp.zeros((BLK, PAD - BLK, 128), jnp.bfloat16)
    for copy in smalls:
        copy.wait()

    row = lax.broadcasted_iota(jnp.int32, (128, 128), 0)
    col = lax.broadcasted_iota(jnp.int32, (128, 128), 1)
    order = (col == row % HALF * 2 + row // HALF).astype(jnp.bfloat16)
    for t in range(4):
        turned = lax.dot_general(
            order, w_proj[:, t * 128 : (t + 1) * 128], (((1,), (1,)), ((), ())), preferred_element_type=jnp.float32
        ).astype(jnp.bfloat16)
        w_wide[t // 2, t % 2 * HALF : (t % 2 + 1) * HALF, :128] = turned[:HALF]
        w_wide[t // 2, t % 2 * HALF : (t % 2 + 1) * HALF, 128:] = turned[HALF:]

    def project(which, msg, part):
        block = wide[pl.ds(part * SUB, SUB)].reshape(SUB * 128, 256)
        both = lax.dot_general(
            w_wide[which], block, (((1,), (1,)), ((), ())), preferred_element_type=jnp.float32
        )
        side = jax.nn.sigmoid(both[:HALF]) * both[HALF:]
        for j in range(SUB):
            stage[pl.ds(j, HALF, stride=SUB), :] = side[:, j * 128 : (j + 1) * 128]
        msg[part] = stage[pl.ds(0, HALF * SUB)].reshape(LAYER, 2 * SUB, 128).astype(jnp.bfloat16)

    def scatter(src_of, dst, send, recv):
        @pl.loop(1, LAYER)
        def _(k):
            ph, pc = peer(k)
            pltpu.make_async_remote_copy(
                src_ref=src_of(ph * 16 + pc), dst_ref=dst, send_sem=send, recv_sem=recv,
                device_id=(2 * z + ph, pc), device_id_type=MESH,
            ).start()

        pltpu.make_async_copy(src_of(me), dst, recv).start()

    def scatter_part(part):
        scatter(lambda n: b_msg.at[part, n], b_in.at[part, me], b_send.at[part], b_recv.at[part])

    def raw_copy(way):
        return pltpu.make_async_remote_copy(
            src_ref=b_msg.at[RAW], dst_ref=raw_in.at[way], send_sem=raw_send.at[way], recv_sem=raw_recv.at[way],
            device_id=beside[way], device_id_type=MESH,
        )

    def whole(ref, sem):
        pltpu.make_async_copy(ref, ref, sem).wait()

    for part in (RAW, 0, 1):
        load(part).wait()
        rows = pl.ds(part * SUB, SUB)
        values = pair[rows].astype(jnp.float32)
        average = jnp.mean(values, axis=-1, keepdims=True)
        centred = values - average
        spread = jnp.mean(centred * centred, axis=-1, keepdims=True)
        result = (centred * lax.rsqrt(spread + epsilon) * ln_gain[...].reshape(1, 1, 128)).astype(jnp.bfloat16)
        normed[rows] = result
        wide[rows, :BLK, :128] = result
        wide[rows, PAD : PAD + BLK, 128:] = result
        project(1, b_msg, part)
        if part == RAW:
            pl.semaphore_wait(barrier, LAYER + 1)
            for way in range(2):
                raw_copy(way).start()
        else:
            scatter_part(part)
    def gathered(into, h, ch):
        rows, lanes = slice(ch // 2 * SUB, (ch // 2 + 1) * SUB), slice(ch % 2 * PAD, ch % 2 * PAD + BLK)
        return jnp.concatenate([into[h * 16 + s, rows, lanes] for s in range(16)], axis=1)

    def gather_into(slot, way, part, into):
        for h in range(2):
            for ch in (2 * way, 2 * way + 1):
                b_all[slot, ch, h, part * SUB : (part + 1) * SUB, :] = gathered(into, h, ch)

    def ring_copy(step, part, way):
        block = pl.ds(2 * way, 2), slice(None), pl.ds(part * SUB, SUB)
        return pltpu.make_async_remote_copy(
            src_ref=b_all.at[(step, *block)], dst_ref=b_all.at[(step + 1, *block)],
            send_sem=ring_send.at[way, step, part], recv_sem=ring_recv.at[way, step, part],
            device_id=beside[way], device_id_type=MESH,
        )

    b_all[:, :, :, BLK:, :] = jnp.zeros((RING, 4, 2, PAD - BLK, K), jnp.bfloat16)
    for part in range(RAW):
        whole(b_in.at[part], b_recv.at[part])
        for way in range(2):
            gather_into(0, way, part, b_in.at[part])
            ring_copy(0, part, way).start()
    for way in range(2):
        raw_copy(way).wait_recv()
        scatter(lambda n: raw_in.at[way, n], raw_all.at[way, me], rest_send.at[way], rest_recv.at[way])

    def sent(step):
        return range(PARTS if 0 < step < RING - 2 else RAW)

    def forward(step):
        for part in sent(step - 1):
            for way in range(2):
                ring_copy(step - 1, part, way).wait_recv()
                if part in sent(step):
                    ring_copy(step, part, way).start()

    low = lax.broadcasted_iota(jnp.int32, (2 * BLK, 128), 1) < PAD

    def multiply(step, way):
        one, two = [
            lax.dot_general(
                a_all[2 * way + i], b_all[step, 2 * way + i].reshape(2 * PAD, K),
                (((1,), (1,)), ((), ())), preferred_element_type=jnp.float32,
            )
            for i in range(2)
        ]
        first = jnp.where(low, one, pltpu.roll(two, PAD, 1)).astype(jnp.bfloat16)
        second = jnp.where(low, pltpu.roll(one, PAD, 1), two).astype(jnp.bfloat16)
        zb = (z + RING - step if way == 0 else z + step) % RING
        for je, value in ((0, first), (1, second)):
            for ih in range(2):
                p_msg[step, way, je, ih] = value[ih * BLK : (ih + 1) * BLK]
                src = p_msg.at[step, way, je, ih]
                dst = p_in.at[me * 2 + way]
                here = jnp.logical_and(ih == xh, 2 * zb + je == c)

                @pl.when(here)
                def _():
                    pltpu.make_async_copy(src, dst, p_recv).start()

                @pl.when(jnp.logical_not(here))
                def _():
                    pltpu.make_async_remote_copy(
                        src_ref=src, dst_ref=dst, send_sem=p_send, recv_sem=p_recv,
                        device_id=(2 * z + ih, 2 * zb + je), device_id_type=MESH,
                    ).start()

    def multiply_both(*steps):
        for step in steps:
            for way in range(2):
                multiply(step, way)

    forward(1)
    scatter_part(RAW)
    for part in range(PARTS):
        project(0, a_msg, part)
    scatter(lambda n: a_msg.at[:, n], a_in.at[:, me], a_send, a_recv)
    for way in range(2):
        whole(raw_all.at[way], rest_recv.at[way])
        gather_into(1, way, RAW, raw_all.at[way])
        ring_copy(1, RAW, way).start()
        gather_into(RING - 1, 1 - way, RAW, raw_all.at[way])
    forward(2)
    whole(b_in.at[RAW], b_recv.at[RAW])
    for way in range(2):
        gather_into(0, way, RAW, b_in.at[RAW])

    @pl.loop(0, PARTS)
    def _(part):
        rows = pl.ds(part * SUB, SUB)
        gate = jnp.dot(normed[rows].reshape(SUB * BLK, 128), w_gate[...], preferred_element_type=jnp.float32)
        gating[rows] = jax.nn.sigmoid(gate).reshape(SUB, BLK, 128)

    forward(3)
    whole(a_in, a_recv)
    for part in range(PARTS):
        for ch in range(4):
            for h in range(2):
                a_all[ch, h * BLK + part * SUB : h * BLK + (part + 1) * SUB, :] = gathered(a_in.at[part], h, ch)
    multiply_both(0, 1)
    forward(4)
    multiply_both(2, 3)
    forward(5)
    multiply_both(4, 5)
    forward(6)
    multiply_both(6)
    for way in range(2):
        for part in sent(RING - 2):
            ring_copy(RING - 2, part, way).wait_recv()
        multiply(RING - 1, way)

    for part in range(PARTS):
        whole(b_msg.at[part, pl.ds(0, LAYER - 1)], b_send.at[part])
    whole(a_msg.at[:, pl.ds(0, LAYER - 1)], a_send)
    for way in range(2):
        raw_copy(way).wait_send()
        whole(raw_in.at[way, pl.ds(0, LAYER - 1)], rest_send.at[way])
        for step in range(RING - 1):
            for part in sent(step):
                ring_copy(step, part, way).wait_send()
    whole(p_in.at[pl.ds(0, 2 * (LAYER - 1))], p_send)
    whole(p_in, p_recv)

    folded = lax.dot_general(order, w_out[...], (((1,), (0,)), ((), ())), preferred_element_type=jnp.float32)
    w_fold[...] = folded.astype(jnp.bfloat16)
    pairs = lax.broadcasted_iota(jnp.int32, (HALF, 128), 0)
    lanes = lax.broadcasted_iota(jnp.int32, (HALF, 128), 1)
    under = lanes < PAD
    picked = [
        jnp.sum(jnp.where(lanes == 2 * pairs + i, out_gain[...], 0.0), axis=1, keepdims=True) for i in range(2)
    ]
    gain[...] = jnp.where(under, picked[0], picked[1])

    @pl.loop(0, PARTS)
    def _(part):
        rows = pl.ds(part * SUB, SUB)
        total = jnp.sum(p_in[:, rows, :].astype(jnp.float32), axis=0)
        average = (total + pltpu.roll(total, PAD, 1)) * (1.0 / 128)
        total = jnp.zeros((SUB, 128), jnp.float32)
        for s in range(HALF):
            centred = p_in[s, rows, :].astype(jnp.float32) - average
            total = total + centred * centred
        spread = (total + pltpu.roll(total, PAD, 1)) * (1.0 / 128)
        factor = lax.rsqrt(spread + epsilon)
        for s in range(HALF):
            centred = p_in[s, rows, :].astype(jnp.float32) - average
            stage[pl.ds(part * SUB + s * BLK, SUB), :] = centred * factor * gain[s : s + 1, :]

    @pl.loop(0, 6)
    def _(n):
        blocks = []
        for i in range(4):
            one = stage[pl.ds(8 * n + 2 * i, HALF, stride=BLK), :]
            two = stage[pl.ds(8 * n + 2 * i + 1, HALF, stride=BLK), :]
            even = jnp.where(under, one, pltpu.roll(two, PAD, 1))
            odd = jnp.where(under, pltpu.roll(one, PAD, 1), two)
            blocks.append(jnp.concatenate([even, odd], axis=0).astype(jnp.bfloat16))
        both = jnp.concatenate(blocks, axis=1)
        result = lax.dot_general(both, w_fold[...], (((0,), (0,)), ((), ())), preferred_element_type=jnp.float32)
        for i in range(8):
            out[8 * n + i] = (gating[8 * n + i] * result[i * PAD : i * PAD + BLK]).astype(jnp.bfloat16)


def per_device(pair, ln_gain, w_proj, w_gate, out_gain, w_out):
    bf16, f32 = jnp.bfloat16, jnp.float32
    vmem = pl.BlockSpec(memory_space=pltpu.VMEM)
    dma = pltpu.SemaphoreType.DMA
    parts = (PARTS, LAYER, 2 * SUB, 128)
    return pl.pallas_call(
        kernel,
        out_shape=jax.ShapeDtypeStruct(pair.shape, bf16),
        in_specs=[pl.BlockSpec(memory_space=pl.ANY)] * 6,
        out_specs=vmem,
        scratch_shapes=[
            pltpu.VMEM((BLK, BLK, 128), bf16),
            pltpu.VMEM((1, 128), f32),
            pltpu.VMEM((128, 512), bf16),
            pltpu.VMEM((128, 128), bf16),
            pltpu.VMEM((1, 128), f32),
            pltpu.VMEM((128, 128), bf16),
            pltpu.VMEM((BLK, BLK, 128), bf16),
            pltpu.VMEM((BLK, 128, 256), bf16),
            pltpu.VMEM((HALF * BLK, 128), f32),
            pltpu.VMEM((BLK, BLK, 128), f32),
            pltpu.VMEM((2, 128, 256), bf16),
            pltpu.VMEM((128, 128), bf16),
            pltpu.VMEM((HALF, 128), f32),
            pltpu.VMEM(parts, bf16),
            pltpu.VMEM(parts, bf16),
            pltpu.VMEM(parts, bf16),
            pltpu.VMEM(parts, bf16),
            pltpu.VMEM((2, *parts[1:]), bf16),
            pltpu.VMEM((2, *parts[1:]), bf16),
            pltpu.VMEM((4, 2 * BLK, K), bf16),
            pltpu.VMEM((RING, 4, 2, PAD, K), bf16),
            pltpu.VMEM((RING, 2, 2, 2, BLK, 128), bf16),
            pltpu.VMEM((2 * LAYER, BLK, 128), bf16),
            dma((PARTS,)), dma((5,)),
            dma((PARTS,)), dma((PARTS,)), dma, dma,
            dma((2,)), dma((2,)), dma((2,)), dma((2,)),
            dma, dma,
            dma((2, RING - 1, PARTS)), dma((2, RING - 1, PARTS)),
        ],
        compiler_params=pltpu.CompilerParams(
            collective_id=0, has_side_effects=True, vmem_limit_bytes=56 * 2**20
        ),
        name="triangle",
    )(pair, ln_gain.reshape(1, 128), w_proj, w_gate, out_gain.reshape(1, 128), w_out)


def solution(mesh):
    in_specs = (P("row", "col", None), P(), P(), P(), P(), P())
    out_specs = P("row", "col", None)
    return jax.shard_map(per_device, mesh=mesh, in_specs=in_specs, out_specs=out_specs, check_vma=False)
```

```python
import jax
import jax.numpy as jnp
from jax import lax
from jax.experimental import pallas as pl
from jax.experimental.pallas import tpu as pltpu
from jax.sharding import PartitionSpec as P

epsilon = 1e-05
MESH = pl.DeviceIdType.MESH
BLK = 48
PAD = 64
HALF = 64
LAYER = 32
RING = 8
K = 768
SUB = 16
PARTS = BLK // SUB
RAW = PARTS - 1


def kernel(
    pair_hbm, ln_gain_hbm, w_proj_hbm, w_gate_hbm, out_gain_hbm, w_out_hbm, out,
    pair, ln_gain, w_proj, w_gate, out_gain, w_out, normed, wide, stage, gating, w_wide, w_fold, gain,
    b_msg, a_msg, b_in, a_in, raw_in, raw_all, a_all, b_all, p_msg, p_in, turned,
    load_sem, small_sem, b_send, b_recv, a_send, a_recv, raw_send, raw_recv, rest_send, rest_recv, p_send, p_recv, ring_send, ring_recv,
):
    r, c = lax.axis_index("row"), lax.axis_index("col")
    z, xh = r // 2, r % 2
    x, y, e = xh * 2 + c // 8, (c // 2) % 4, c % 2
    me = xh * 16 + c

    def load(part):
        rows = pl.ds(part * SUB, SUB)
        return pltpu.make_async_copy(pair_hbm.at[rows], pair.at[rows], load_sem.at[part])

    smalls = [
        pltpu.make_async_copy(src, dst, small_sem.at[i])
        for i, (src, dst) in enumerate((
            (w_proj_hbm, w_proj), (ln_gain_hbm, ln_gain), (w_gate_hbm, w_gate),
            (out_gain_hbm, out_gain), (w_out_hbm, w_out),
        ))
    ]
    smalls[0].start()
    for part in range(PARTS):
        load(part).start()
    for copy in smalls[1:]:
        copy.start()

    def peer(k):
        k = k + e * (LAYER - 2 * k)
        t = (11 * k) % LAYER
        px, py, pe = (x + t // 8) % 4, (y + (t // 2) % 4) % 4, (e + t % 2) % 2
        return px // 2, (px % 2) * 8 + py * 2 + pe

    beside = (((z + 1) % RING * 2 + xh, c), ((z + RING - 1) % RING * 2 + xh, c))

    barrier = pltpu.get_barrier_semaphore()

    @pl.loop(1, LAYER)
    def _(k):
        ph, pc = peer(k)
        pl.semaphore_signal(barrier, inc=1, device_id=(2 * z + ph, pc), device_id_type=MESH)

    for way in range(2):
        pl.semaphore_signal(barrier, inc=1, device_id=beside[way], device_id_type=MESH)

    wide[:, :, 128:] = jnp.zeros((BLK, 128, 128), jnp.bfloat16)
    wide[:, PAD:, :128] = jnp.zeros((BLK, PAD, 128), jnp.bfloat16)
    wide[:, BLK:PAD, :128] = jnp.zeros((BLK, PAD - BLK, 128), jnp.bfloat16)
    for copy in smalls:
        copy.wait()

    row = lax.broadcasted_iota(jnp.int32, (128, 128), 0)
    col = lax.broadcasted_iota(jnp.int32, (128, 128), 1)
    order = (col == row % HALF * 2 + row // HALF).astype(jnp.bfloat16)
    for t in range(4):
        mixed = lax.dot_general(
            order, w_proj[:, t * 128 : (t + 1) * 128], (((1,), (1,)), ((), ())), preferred_element_type=jnp.float32
        ).astype(jnp.bfloat16)
        w_wide[t // 2, t % 2 * HALF : (t % 2 + 1) * HALF, :128] = mixed[:HALF]
        w_wide[t // 2, t % 2 * HALF : (t % 2 + 1) * HALF, 128:] = mixed[HALF:]

    def project(which, msg, part):
        block = wide[pl.ds(part * SUB, SUB)].reshape(SUB * 128, 256)
        both = lax.dot_general(
            w_wide[which], block, (((1,), (1,)), ((), ())), preferred_element_type=jnp.float32
        )
        side = jax.nn.sigmoid(both[:HALF]) * both[HALF:]
        for j in range(SUB):
            stage[pl.ds(j, HALF, stride=SUB), :] = side[:, j * 128 : (j + 1) * 128]
        msg[part] = stage[pl.ds(0, HALF * SUB)].reshape(LAYER, 2 * SUB, 128).astype(jnp.bfloat16)

    def scatter(src_of, dst, send, recv):
        @pl.loop(1, LAYER)
        def _(k):
            ph, pc = peer(k)
            pltpu.make_async_remote_copy(
                src_ref=src_of(ph * 16 + pc), dst_ref=dst, send_sem=send, recv_sem=recv,
                device_id=(2 * z + ph, pc), device_id_type=MESH,
            ).start()

        pltpu.make_async_copy(src_of(me), dst, recv).start()

    def scatter_part(part):
        scatter(lambda n: b_msg.at[part, n], b_in.at[part, me], b_send.at[part], b_recv.at[part])

    def raw_copy(way):
        return pltpu.make_async_remote_copy(
            src_ref=b_msg.at[RAW], dst_ref=raw_in.at[way], send_sem=raw_send.at[way], recv_sem=raw_recv.at[way],
            device_id=beside[way], device_id_type=MESH,
        )

    def whole(ref, sem):
        pltpu.make_async_copy(ref, ref, sem).wait()

    for part in (RAW, 0, 1):
        load(part).wait()
        rows = pl.ds(part * SUB, SUB)
        values = pair[rows].astype(jnp.float32)
        average = jnp.mean(values, axis=-1, keepdims=True)
        centred = values - average
        spread = jnp.mean(centred * centred, axis=-1, keepdims=True)
        result = (centred * lax.rsqrt(spread + epsilon) * ln_gain[...].reshape(1, 1, 128)).astype(jnp.bfloat16)
        normed[rows] = result
        wide[rows, :BLK, :128] = result
        wide[rows, PAD : PAD + BLK, 128:] = result
        project(1, b_msg, part)
        if part == RAW:
            pl.semaphore_wait(barrier, LAYER + 1)
            for way in range(2):
                raw_copy(way).start()
        else:
            scatter_part(part)
    def gathered(into, h, ch):
        rows, lanes = slice(ch // 2 * SUB, (ch // 2 + 1) * SUB), slice(ch % 2 * PAD, ch % 2 * PAD + BLK)
        return jnp.concatenate([into[h * 16 + s, rows, lanes] for s in range(16)], axis=1)

    def gather_into(slot, way, part, into):
        for h in range(2):
            for ch in (2 * way, 2 * way + 1):
                b_all[slot, ch, h, part * SUB : (part + 1) * SUB, :] = gathered(into, h, ch)

    def ring_copy(step, part, way):
        block = pl.ds(2 * way, 2), slice(None), pl.ds(part * SUB, SUB)
        return pltpu.make_async_remote_copy(
            src_ref=b_all.at[(step, *block)], dst_ref=b_all.at[(step + 1, *block)],
            send_sem=ring_send.at[way, step, part], recv_sem=ring_recv.at[way, step, part],
            device_id=beside[way], device_id_type=MESH,
        )

    a_all[:, :, BLK:, :] = jnp.zeros((4, 2, PAD - BLK, K), jnp.bfloat16)
    for part in range(RAW):
        whole(b_in.at[part], b_recv.at[part])
        for way in range(2):
            gather_into(0, way, part, b_in.at[part])
            ring_copy(0, part, way).start()
    for way in range(2):
        raw_copy(way).wait_recv()
        scatter(lambda n: raw_in.at[way, n], raw_all.at[way, me], rest_send.at[way], rest_recv.at[way])

    def sent(step):
        return range(PARTS if 0 < step < RING - 2 else RAW)

    def forward(step):
        for part in sent(step - 1):
            for way in range(2):
                ring_copy(step - 1, part, way).wait_recv()
                if part in sent(step):
                    ring_copy(step, part, way).start()

    def multiply(step, way, part=None):
        count, begin = (BLK, 0) if part is None else (SUB, part * SUB)
        rows = slice(begin, begin + count)
        one, two = [
            lax.dot_general(
                b_all[step, ch, :, rows, :].reshape(2 * count, K), a_all[ch].reshape(2 * PAD, K),
                (((1,), (1,)), ((), ())), preferred_element_type=jnp.float32,
            )
            for ch in (2 * way, 2 * way + 1)
        ]
        low = lax.broadcasted_iota(jnp.int32, (2 * count, 128), 1) < PAD
        first = jnp.where(low, one, pltpu.roll(two, PAD, 1)).astype(jnp.bfloat16)
        second = jnp.where(low, pltpu.roll(one, PAD, 1), two).astype(jnp.bfloat16)
        zb = (z + RING - step if way == 0 else z + step) % RING
        for ih, value in ((0, first), (1, second)):
            for je in range(2):
                p_msg[step, way, je, ih, rows, :] = value[je * count : (je + 1) * count]
                src = p_msg.at[step, way, je, ih, pl.ds(begin, count)]
                dst = p_in.at[me + LAYER * way, pl.ds(begin, count)]
                recv = p_recv.at[PARTS + way if part is None else part]
                here = jnp.logical_and(ih == xh, 2 * zb + je == c)

                @pl.when(here)
                def _():
                    pltpu.make_async_copy(src, dst, recv).start()

                @pl.when(jnp.logical_not(here))
                def _():
                    pltpu.make_async_remote_copy(
                        src_ref=src, dst_ref=dst, send_sem=p_send, recv_sem=recv,
                        device_id=(2 * z + ih, 2 * zb + je), device_id_type=MESH,
                    ).start()

    def multiply_both(*steps):
        for step in steps:
            for way in range(2):
                multiply(step, way)

    forward(1)
    scatter_part(RAW)
    for part in range(PARTS):
        project(0, a_msg, part)
    scatter(lambda n: a_msg.at[:, n], a_in.at[:, me], a_send, a_recv)
    for way in range(2):
        whole(raw_all.at[way], rest_recv.at[way])
        gather_into(1, way, RAW, raw_all.at[way])
        ring_copy(1, RAW, way).start()
        gather_into(RING - 1, 1 - way, RAW, raw_all.at[way])
    forward(2)
    whole(b_in.at[RAW], b_recv.at[RAW])
    for way in range(2):
        gather_into(0, way, RAW, b_in.at[RAW])

    folded = lax.dot_general(order, w_out[...], (((1,), (0,)), ((), ())), preferred_element_type=jnp.float32)
    w_fold[...] = folded.astype(jnp.bfloat16)
    pairs = lax.broadcasted_iota(jnp.int32, (HALF, 128), 0)
    lanes = lax.broadcasted_iota(jnp.int32, (HALF, 128), 1)
    under = lanes < PAD
    picked = [
        jnp.sum(jnp.where(lanes == 2 * pairs + i, out_gain[...], 0.0), axis=1, keepdims=True) for i in range(2)
    ]
    gain[...] = jnp.where(under, picked[0], picked[1])

    @pl.loop(0, PARTS)
    def _(part):
        rows = pl.ds(part * SUB, SUB)
        gate = jnp.dot(normed[rows].reshape(SUB * BLK, 128), w_gate[...], preferred_element_type=jnp.float32)
        gating[rows] = jax.nn.sigmoid(gate).reshape(SUB, BLK, 128)

    forward(3)
    whole(a_in, a_recv)
    for part in range(PARTS):
        for ch in range(4):
            for h in range(2):
                a_all[ch, h, part * SUB : (part + 1) * SUB, :] = gathered(a_in.at[part], h, ch)
    multiply_both(0, 1)
    forward(4)
    multiply_both(2, 3)
    forward(5)
    multiply_both(4, 5)
    forward(6)
    multiply_both(6)
    for way in range(2):
        multiply(RING - 1, way, RAW)
    for part in sent(RING - 2):
        for way in range(2):
            ring_copy(RING - 2, part, way).wait_recv()
            multiply(RING - 1, way, part)

    distance = (z + RING - c // 2) % RING
    for way in range(2):
        last = distance == (RING - 1 if way == 0 else 1)

        @pl.when(jnp.logical_not(last))
        def _():
            whole(p_in.at[pl.ds(LAYER * way, LAYER)], p_recv.at[PARTS + way])

    for part in (RAW, *sent(RING - 2)):
        rows = pl.ds(part * SUB, SUB)
        for way in range(2):
            last = distance == (RING - 1 if way == 0 else 1)

            @pl.when(last)
            def _():
                whole(p_in.at[pl.ds(LAYER * way, LAYER), rows], p_recv.at[part])

        slots = [n // 2 + LAYER * (n % 2) for n in range(HALF)]
        total = jnp.zeros((SUB, 128), jnp.float32)
        for s in slots:
            total = total + p_in[s, rows, :].astype(jnp.float32)
        average = (total + pltpu.roll(total, PAD, 1)) * (1.0 / 128)
        total = jnp.zeros((SUB, 128), jnp.float32)
        for s in slots:
            centred = p_in[s, rows, :].astype(jnp.float32) - average
            total = total + centred * centred
        spread = (total + pltpu.roll(total, PAD, 1)) * (1.0 / 128)
        factor = lax.rsqrt(spread + epsilon)
        for n, s in enumerate(slots):
            centred = p_in[s, rows, :].astype(jnp.float32) - average
            stage[n * SUB : (n + 1) * SUB, :] = centred * factor * gain[n : n + 1, :]

        for n in range(2):
            blocks = []
            for i in range(4):
                one = stage[pl.ds(8 * n + 2 * i, HALF, stride=SUB), :]
                two = stage[pl.ds(8 * n + 2 * i + 1, HALF, stride=SUB), :]
                even = jnp.where(under, one, pltpu.roll(two, PAD, 1))
                odd = jnp.where(under, pltpu.roll(one, PAD, 1), two)
                blocks.append(jnp.concatenate([even, odd], axis=0).astype(jnp.bfloat16))
            both = jnp.concatenate(blocks, axis=1)
            result = lax.dot_general(
                both, w_fold[...], (((0,), (0,)), ((), ())), preferred_element_type=jnp.float32
            )
            for j in range(8):
                turned[pl.ds(part * SUB + 8 * n + j, BLK, stride=BLK), :] = result[j * PAD : j * PAD + BLK]

    @pl.loop(0, PARTS)
    def _(part):
        rows = pl.ds(part * SUB, SUB)
        result = turned[pl.ds(part * SUB * BLK, SUB * BLK), :].reshape(SUB, BLK, 128)
        out[rows] = (gating[rows] * result).astype(jnp.bfloat16)

    for part in range(PARTS):
        whole(b_msg.at[part, pl.ds(0, LAYER - 1)], b_send.at[part])
    whole(a_msg.at[:, pl.ds(0, LAYER - 1)], a_send)
    whole(p_in.at[pl.ds(0, 2 * (LAYER - 1))], p_send)
    for way in range(2):
        raw_copy(way).wait_send()
        whole(raw_in.at[way, pl.ds(0, LAYER - 1)], rest_send.at[way])
        for step in range(RING - 1):
            for part in sent(step):
                ring_copy(step, part, way).wait_send()


def per_device(pair, ln_gain, w_proj, w_gate, out_gain, w_out):
    bf16, f32 = jnp.bfloat16, jnp.float32
    vmem = pl.BlockSpec(memory_space=pltpu.VMEM)
    dma = pltpu.SemaphoreType.DMA
    parts = (PARTS, LAYER, 2 * SUB, 128)
    return pl.pallas_call(
        kernel,
        out_shape=jax.ShapeDtypeStruct(pair.shape, bf16),
        in_specs=[pl.BlockSpec(memory_space=pl.ANY)] * 6,
        out_specs=vmem,
        scratch_shapes=[
            pltpu.VMEM((BLK, BLK, 128), bf16),
            pltpu.VMEM((1, 128), f32),
            pltpu.VMEM((128, 512), bf16),
            pltpu.VMEM((128, 128), bf16),
            pltpu.VMEM((1, 128), f32),
            pltpu.VMEM((128, 128), bf16),
            pltpu.VMEM((BLK, BLK, 128), bf16),
            pltpu.VMEM((BLK, 128, 256), bf16),
            pltpu.VMEM((HALF * BLK, 128), f32),
            pltpu.VMEM((BLK, BLK, 128), f32),
            pltpu.VMEM((2, 128, 256), bf16),
            pltpu.VMEM((128, 128), bf16),
            pltpu.VMEM((HALF, 128), f32),
            pltpu.VMEM(parts, bf16),
            pltpu.VMEM(parts, bf16),
            pltpu.VMEM(parts, bf16),
            pltpu.VMEM(parts, bf16),
            pltpu.VMEM((2, *parts[1:]), bf16),
            pltpu.VMEM((2, *parts[1:]), bf16),
            pltpu.VMEM((4, 2, PAD, K), bf16),
            pltpu.VMEM((RING, 4, 2, BLK, K), bf16),
            pltpu.VMEM((RING, 2, 2, 2, BLK, 128), bf16),
            pltpu.VMEM((2 * LAYER, BLK, 128), bf16),
            pltpu.VMEM((BLK * BLK, 128), f32),
            dma((PARTS,)), dma((5,)),
            dma((PARTS,)), dma((PARTS,)), dma, dma,
            dma((2,)), dma((2,)), dma((2,)), dma((2,)),
            dma, dma((PARTS + 2,)),
            dma((2, RING - 1, PARTS)), dma((2, RING - 1, PARTS)),
        ],
        compiler_params=pltpu.CompilerParams(
            collective_id=0, has_side_effects=True, vmem_limit_bytes=56 * 2**20
        ),
        name="triangle",
    )(pair, ln_gain.reshape(1, 128), w_proj, w_gate, out_gain.reshape(1, 128), w_out)


def solution(mesh):
    in_specs = (P("row", "col", None), P(), P(), P(), P(), P())
    out_specs = P("row", "col", None)
    return jax.shard_map(per_device, mesh=mesh, in_specs=in_specs, out_specs=out_specs, check_vma=False)
```

```python
import jax
import jax.numpy as jnp
from jax import lax
from jax.experimental import pallas as pl
from jax.experimental.pallas import tpu as pltpu
from jax.sharding import PartitionSpec as P

epsilon = 1e-05
MESH = pl.DeviceIdType.MESH
BLK = 48
PAD = 64
HALF = 64
LAYER = 32
RING = 8
K = 768
SUB = 16
PARTS = BLK // SUB
RAW = PARTS - 1


OFFSETS = [(2, 2, 0), (2, 2, 1), (2, 3, 0), (2, 3, 1), (3, 2, 0), (3, 2, 1), (2, 1, 0), (2, 1, 1), (1, 2, 0), (1, 2, 1), (2, 0, 0), (2, 0, 1), (0, 2, 0), (0, 2, 1), (3, 1, 0), (3, 1, 1), (1, 3, 0), (1, 3, 1), (3, 3, 0), (3, 3, 1), (1, 1, 0), (1, 1, 1), (3, 0, 0), (3, 0, 1), (0, 3, 0), (0, 3, 1), (1, 0, 0), (1, 0, 1), (0, 1, 0), (0, 1, 1), (0, 0, 1)]


def kernel(
    pair_hbm, ln_gain_hbm, w_proj_hbm, w_gate_hbm, out_gain_hbm, w_out_hbm, out,
    pair, ln_gain, w_proj, w_gate, out_gain, w_out, normed, wide, stage, gating, w_wide, w_fold, gain,
    b_msg, a_msg, b_in, a_in, raw_in, raw_all, a_all, b_all, p_msg, p_in, turned,
    load_sem, small_sem, b_send, b_recv, a_send, a_recv, raw_send, raw_recv, rest_send, rest_recv, p_send, p_recv, ring_send, ring_recv,
):
    r, c = lax.axis_index("row"), lax.axis_index("col")
    z, xh = r // 2, r % 2
    x, y, e = xh * 2 + c // 8, (c // 2) % 4, c % 2
    me = xh * 16 + c

    def load(part):
        rows = pl.ds(part * SUB, SUB)
        return pltpu.make_async_copy(pair_hbm.at[rows], pair.at[rows], load_sem.at[part])

    smalls = [
        pltpu.make_async_copy(src, dst, small_sem.at[i])
        for i, (src, dst) in enumerate((
            (w_proj_hbm, w_proj), (ln_gain_hbm, ln_gain), (w_gate_hbm, w_gate),
            (out_gain_hbm, out_gain), (w_out_hbm, w_out),
        ))
    ]
    smalls[0].start()
    for part in range(PARTS):
        load(part).start()
    for copy in smalls[1:]:
        copy.start()

    def peer(k):
        dx, dy, de = OFFSETS[k]
        px, py, pe = (x + dx) % 4, (y + dy) % 4, (e + de) % 2
        return px // 2, (px % 2) * 8 + py * 2 + pe

    beside = (((z + 1) % RING * 2 + xh, c), ((z + RING - 1) % RING * 2 + xh, c))

    barrier = pltpu.get_barrier_semaphore()

    for k in range(LAYER - 1):
        ph, pc = peer(k)
        pl.semaphore_signal(barrier, inc=1, device_id=(2 * z + ph, pc), device_id_type=MESH)

    for way in range(2):
        pl.semaphore_signal(barrier, inc=1, device_id=beside[way], device_id_type=MESH)

    wide[:, :, 128:] = jnp.zeros((BLK, 128, 128), jnp.bfloat16)
    wide[:, PAD:, :128] = jnp.zeros((BLK, PAD, 128), jnp.bfloat16)
    wide[:, BLK:PAD, :128] = jnp.zeros((BLK, PAD - BLK, 128), jnp.bfloat16)
    for copy in smalls:
        copy.wait()

    row = lax.broadcasted_iota(jnp.int32, (128, 128), 0)
    col = lax.broadcasted_iota(jnp.int32, (128, 128), 1)
    order = (col == row % HALF * 2 + row // HALF).astype(jnp.bfloat16)
    for t in range(4):
        mixed = lax.dot_general(
            order, w_proj[:, t * 128 : (t + 1) * 128], (((1,), (1,)), ((), ())), preferred_element_type=jnp.float32
        ).astype(jnp.bfloat16)
        w_wide[t // 2, t % 2 * HALF : (t % 2 + 1) * HALF, :128] = mixed[:HALF]
        w_wide[t // 2, t % 2 * HALF : (t % 2 + 1) * HALF, 128:] = mixed[HALF:]

    def project(which, msg, part):
        block = wide[pl.ds(part * SUB, SUB)].reshape(SUB * 128, 256)
        both = lax.dot_general(
            w_wide[which], block, (((1,), (1,)), ((), ())), preferred_element_type=jnp.float32
        )
        side = jax.nn.sigmoid(both[:HALF]) * both[HALF:]
        for j in range(SUB):
            stage[pl.ds(j, HALF, stride=SUB), :] = side[:, j * 128 : (j + 1) * 128]
        msg[part] = stage[pl.ds(0, HALF * SUB)].reshape(LAYER, 2 * SUB, 128).astype(jnp.bfloat16)

    def scatter(src_of, dst, send, recv):
        for k in range(LAYER - 1):
            ph, pc = peer(k)
            pltpu.make_async_remote_copy(
                src_ref=src_of(ph * 16 + pc), dst_ref=dst, send_sem=send, recv_sem=recv,
                device_id=(2 * z + ph, pc), device_id_type=MESH,
            ).start()

        pltpu.make_async_copy(src_of(me), dst, recv).start()

    def scatter_part(part):
        scatter(lambda n: b_msg.at[part, n], b_in.at[part, me], b_send.at[part], b_recv.at[part])

    def raw_copy(way):
        return pltpu.make_async_remote_copy(
            src_ref=b_msg.at[RAW], dst_ref=raw_in.at[way], send_sem=raw_send.at[way], recv_sem=raw_recv.at[way],
            device_id=beside[way], device_id_type=MESH,
        )

    def whole(ref, sem):
        pltpu.make_async_copy(ref, ref, sem).wait()

    for part in (RAW, 0, 1):
        load(part).wait()
        rows = pl.ds(part * SUB, SUB)
        values = pair[rows].astype(jnp.float32)
        average = jnp.mean(values, axis=-1, keepdims=True)
        centred = values - average
        spread = jnp.mean(centred * centred, axis=-1, keepdims=True)
        result = (centred * lax.rsqrt(spread + epsilon) * ln_gain[...].reshape(1, 1, 128)).astype(jnp.bfloat16)
        normed[rows] = result
        wide[rows, :BLK, :128] = result
        wide[rows, PAD : PAD + BLK, 128:] = result
        project(1, b_msg, part)
        if part == RAW:
            pl.semaphore_wait(barrier, LAYER + 1)
            for way in range(2):
                raw_copy(way).start()
        else:
            scatter_part(part)
    def gathered(into, h, ch):
        rows, lanes = slice(ch // 2 * SUB, (ch // 2 + 1) * SUB), slice(ch % 2 * PAD, ch % 2 * PAD + BLK)
        return jnp.concatenate([into[h * 16 + s, rows, lanes] for s in range(16)], axis=1)

    def gather_into(slot, way, part, into):
        for h in range(2):
            for ch in (2 * way, 2 * way + 1):
                b_all[slot, ch, h, part * SUB : (part + 1) * SUB, :] = gathered(into, h, ch)

    def ring_copy(step, part, way):
        block = pl.ds(2 * way, 2), slice(None), pl.ds(part * SUB, SUB)
        return pltpu.make_async_remote_copy(
            src_ref=b_all.at[(step, *block)], dst_ref=b_all.at[(step + 1, *block)],
            send_sem=ring_send.at[way, step, part], recv_sem=ring_recv.at[way, step, part],
            device_id=beside[way], device_id_type=MESH,
        )

    a_all[:, :, BLK:, :] = jnp.zeros((4, 2, PAD - BLK, K), jnp.bfloat16)
    for part in range(RAW):
        whole(b_in.at[part], b_recv.at[part])
        for way in range(2):
            gather_into(0, way, part, b_in.at[part])
            ring_copy(0, part, way).start()
    for way in range(2):
        raw_copy(way).wait_recv()
        scatter(lambda n: raw_in.at[way, n], raw_all.at[way, me], rest_send.at[way], rest_recv.at[way])

    def sent(step):
        return range(PARTS if 0 < step < RING - 2 else RAW)

    def forward(step):
        for part in sent(step - 1):
            for way in range(2):
                ring_copy(step - 1, part, way).wait_recv()
                if part in sent(step):
                    ring_copy(step, part, way).start()

    def multiply(step, way, part=None):
        count, begin = (BLK, 0) if part is None else (SUB, part * SUB)
        rows = slice(begin, begin + count)
        one, two = [
            lax.dot_general(
                b_all[step, ch, :, rows, :].reshape(2 * count, K), a_all[ch].reshape(2 * PAD, K),
                (((1,), (1,)), ((), ())), preferred_element_type=jnp.float32,
            )
            for ch in (2 * way, 2 * way + 1)
        ]
        low = lax.broadcasted_iota(jnp.int32, (2 * count, 128), 1) < PAD
        first = jnp.where(low, one, pltpu.roll(two, PAD, 1)).astype(jnp.bfloat16)
        second = jnp.where(low, pltpu.roll(one, PAD, 1), two).astype(jnp.bfloat16)
        zb = (z + RING - step if way == 0 else z + step) % RING
        for ih, value in ((0, first), (1, second)):
            for je in range(2):
                p_msg[step, way, je, ih, rows, :] = value[je * count : (je + 1) * count]
                src = p_msg.at[step, way, je, ih, pl.ds(begin, count)]
                dst = p_in.at[me + LAYER * way, pl.ds(begin, count)]
                recv = p_recv.at[PARTS + way if part is None else part]
                here = jnp.logical_and(ih == xh, 2 * zb + je == c)

                @pl.when(here)
                def _():
                    pltpu.make_async_copy(src, dst, recv).start()

                @pl.when(jnp.logical_not(here))
                def _():
                    pltpu.make_async_remote_copy(
                        src_ref=src, dst_ref=dst, send_sem=p_send, recv_sem=recv,
                        device_id=(2 * z + ih, 2 * zb + je), device_id_type=MESH,
                    ).start()

    def multiply_both(*steps):
        for step in steps:
            for way in range(2):
                multiply(step, way)

    forward(1)
    scatter_part(RAW)
    for part in range(PARTS):
        project(0, a_msg, part)
    scatter(lambda n: a_msg.at[:, n], a_in.at[:, me], a_send, a_recv)
    for way in range(2):
        whole(raw_all.at[way], rest_recv.at[way])
        gather_into(1, way, RAW, raw_all.at[way])
        ring_copy(1, RAW, way).start()
        gather_into(RING - 1, 1 - way, RAW, raw_all.at[way])
    forward(2)
    whole(b_in.at[RAW], b_recv.at[RAW])
    for way in range(2):
        gather_into(0, way, RAW, b_in.at[RAW])

    folded = lax.dot_general(order, w_out[...], (((1,), (0,)), ((), ())), preferred_element_type=jnp.float32)
    w_fold[...] = folded.astype(jnp.bfloat16)
    pairs = lax.broadcasted_iota(jnp.int32, (HALF, 128), 0)
    lanes = lax.broadcasted_iota(jnp.int32, (HALF, 128), 1)
    under = lanes < PAD
    picked = [
        jnp.sum(jnp.where(lanes == 2 * pairs + i, out_gain[...], 0.0), axis=1, keepdims=True) for i in range(2)
    ]
    gain[...] = jnp.where(under, picked[0], picked[1])

    @pl.loop(0, PARTS)
    def _(part):
        rows = pl.ds(part * SUB, SUB)
        gate = jnp.dot(normed[rows].reshape(SUB * BLK, 128), w_gate[...], preferred_element_type=jnp.float32)
        gating[rows] = jax.nn.sigmoid(gate).reshape(SUB, BLK, 128)

    forward(3)
    whole(a_in, a_recv)
    for part in range(PARTS):
        for ch in range(4):
            for h in range(2):
                a_all[ch, h, part * SUB : (part + 1) * SUB, :] = gathered(a_in.at[part], h, ch)
    multiply_both(0, 1)
    forward(4)
    multiply_both(2, 3)
    forward(5)
    multiply_both(4, 5)
    forward(6)
    multiply_both(6)
    for way in range(2):
        multiply(RING - 1, way, RAW)
    for part in sent(RING - 2):
        for way in range(2):
            ring_copy(RING - 2, part, way).wait_recv()
            multiply(RING - 1, way, part)

    distance = (z + RING - c // 2) % RING
    for way in range(2):
        last = distance == (RING - 1 if way == 0 else 1)

        @pl.when(jnp.logical_not(last))
        def _():
            whole(p_in.at[pl.ds(LAYER * way, LAYER)], p_recv.at[PARTS + way])

    for part in (RAW, *sent(RING - 2)):
        rows = pl.ds(part * SUB, SUB)
        for way in range(2):
            last = distance == (RING - 1 if way == 0 else 1)

            @pl.when(last)
            def _():
                whole(p_in.at[pl.ds(LAYER * way, LAYER), rows], p_recv.at[part])

        slots = [n // 2 + LAYER * (n % 2) for n in range(HALF)]
        total = jnp.zeros((SUB, 128), jnp.float32)
        for s in slots:
            total = total + p_in[s, rows, :].astype(jnp.float32)
        average = (total + pltpu.roll(total, PAD, 1)) * (1.0 / 128)
        total = jnp.zeros((SUB, 128), jnp.float32)
        for s in slots:
            centred = p_in[s, rows, :].astype(jnp.float32) - average
            total = total + centred * centred
        spread = (total + pltpu.roll(total, PAD, 1)) * (1.0 / 128)
        factor = lax.rsqrt(spread + epsilon)
        for n, s in enumerate(slots):
            centred = p_in[s, rows, :].astype(jnp.float32) - average
            stage[n * SUB : (n + 1) * SUB, :] = centred * factor * gain[n : n + 1, :]

        for n in range(2):
            blocks = []
            for i in range(4):
                one = stage[pl.ds(8 * n + 2 * i, HALF, stride=SUB), :]
                two = stage[pl.ds(8 * n + 2 * i + 1, HALF, stride=SUB), :]
                even = jnp.where(under, one, pltpu.roll(two, PAD, 1))
                odd = jnp.where(under, pltpu.roll(one, PAD, 1), two)
                blocks.append(jnp.concatenate([even, odd], axis=0).astype(jnp.bfloat16))
            both = jnp.concatenate(blocks, axis=1)
            result = lax.dot_general(
                both, w_fold[...], (((0,), (0,)), ((), ())), preferred_element_type=jnp.float32
            )
            for j in range(8):
                turned[pl.ds(part * SUB + 8 * n + j, BLK, stride=BLK), :] = result[j * PAD : j * PAD + BLK]

    @pl.loop(0, PARTS)
    def _(part):
        rows = pl.ds(part * SUB, SUB)
        result = turned[pl.ds(part * SUB * BLK, SUB * BLK), :].reshape(SUB, BLK, 128)
        out[rows] = (gating[rows] * result).astype(jnp.bfloat16)

    for part in range(PARTS):
        whole(b_msg.at[part, pl.ds(0, LAYER - 1)], b_send.at[part])
    whole(a_msg.at[:, pl.ds(0, LAYER - 1)], a_send)
    whole(p_in.at[pl.ds(0, 2 * (LAYER - 1))], p_send)
    for way in range(2):
        raw_copy(way).wait_send()
        whole(raw_in.at[way, pl.ds(0, LAYER - 1)], rest_send.at[way])
        for step in range(RING - 1):
            for part in sent(step):
                ring_copy(step, part, way).wait_send()


def per_device(pair, ln_gain, w_proj, w_gate, out_gain, w_out):
    bf16, f32 = jnp.bfloat16, jnp.float32
    vmem = pl.BlockSpec(memory_space=pltpu.VMEM)
    dma = pltpu.SemaphoreType.DMA
    parts = (PARTS, LAYER, 2 * SUB, 128)
    return pl.pallas_call(
        kernel,
        out_shape=jax.ShapeDtypeStruct(pair.shape, bf16),
        in_specs=[pl.BlockSpec(memory_space=pl.ANY)] * 6,
        out_specs=vmem,
        scratch_shapes=[
            pltpu.VMEM((BLK, BLK, 128), bf16),
            pltpu.VMEM((1, 128), f32),
            pltpu.VMEM((128, 512), bf16),
            pltpu.VMEM((128, 128), bf16),
            pltpu.VMEM((1, 128), f32),
            pltpu.VMEM((128, 128), bf16),
            pltpu.VMEM((BLK, BLK, 128), bf16),
            pltpu.VMEM((BLK, 128, 256), bf16),
            pltpu.VMEM((HALF * BLK, 128), f32),
            pltpu.VMEM((BLK, BLK, 128), f32),
            pltpu.VMEM((2, 128, 256), bf16),
            pltpu.VMEM((128, 128), bf16),
            pltpu.VMEM((HALF, 128), f32),
            pltpu.VMEM(parts, bf16),
            pltpu.VMEM(parts, bf16),
            pltpu.VMEM(parts, bf16),
            pltpu.VMEM(parts, bf16),
            pltpu.VMEM((2, *parts[1:]), bf16),
            pltpu.VMEM((2, *parts[1:]), bf16),
            pltpu.VMEM((4, 2, PAD, K), bf16),
            pltpu.VMEM((RING, 4, 2, BLK, K), bf16),
            pltpu.VMEM((RING, 2, 2, 2, BLK, 128), bf16),
            pltpu.VMEM((2 * LAYER, BLK, 128), bf16),
            pltpu.VMEM((BLK * BLK, 128), f32),
            dma((PARTS,)), dma((5,)),
            dma((PARTS,)), dma((PARTS,)), dma, dma,
            dma((2,)), dma((2,)), dma((2,)), dma((2,)),
            dma, dma((PARTS + 2,)),
            dma((2, RING - 1, PARTS)), dma((2, RING - 1, PARTS)),
        ],
        compiler_params=pltpu.CompilerParams(
            collective_id=0, has_side_effects=True, vmem_limit_bytes=56 * 2**20
        ),
        name="triangle",
    )(pair, ln_gain.reshape(1, 128), w_proj, w_gate, out_gain.reshape(1, 128), w_out)


def solution(mesh):
    in_specs = (P("row", "col", None), P(), P(), P(), P(), P())
    out_specs = P("row", "col", None)
    return jax.shard_map(per_device, mesh=mesh, in_specs=in_specs, out_specs=out_specs, check_vma=False)
```

```python
import jax
import jax.numpy as jnp
from jax import lax
from jax.experimental import pallas as pl
from jax.experimental.pallas import tpu as pltpu
from jax.sharding import PartitionSpec as P

epsilon = 1e-05
MESH = pl.DeviceIdType.MESH
BLK = 48
PAD = 64
HALF = 64
LAYER = 32
RING = 8
K = 768
SUB = 16
PARTS = BLK // SUB
RAW = PARTS - 1


OFFSETS = [(2, 2, 0), (2, 2, 1), (2, 3, 0), (2, 3, 1), (3, 2, 0), (3, 2, 1), (2, 1, 0), (2, 1, 1), (1, 2, 0), (1, 2, 1), (2, 0, 0), (2, 0, 1), (0, 2, 0), (0, 2, 1), (3, 1, 0), (3, 1, 1), (1, 3, 0), (1, 3, 1), (3, 3, 0), (3, 3, 1), (1, 1, 0), (1, 1, 1), (3, 0, 0), (3, 0, 1), (0, 3, 0), (0, 3, 1), (1, 0, 0), (1, 0, 1), (0, 1, 0), (0, 1, 1), (0, 0, 1)]


def kernel(
    pair_hbm, ln_gain_hbm, w_proj_hbm, w_gate_hbm, out_gain_hbm, w_out_hbm, out,
    pair, ln_gain, w_proj, w_gate, out_gain, w_out, normed, wide, stage, gating, w_wide, w_fold, gain,
    b_msg, a_msg, b_in, a_in, raw_in, raw_all, a_all, b_all, p_msg, p_in, turned,
    load_sem, small_sem, b_send, b_recv, a_send, a_recv, raw_send, raw_recv, rest_send, rest_recv, p_send, p_recv, ring_send, ring_recv,
):
    r, c = lax.axis_index("row"), lax.axis_index("col")
    z, xh = r // 2, r % 2
    x, y, e = xh * 2 + c // 8, (c // 2) % 4, c % 2
    me = xh * 16 + c

    def load(part):
        rows = pl.ds(part * SUB, SUB)
        return pltpu.make_async_copy(pair_hbm.at[rows], pair.at[rows], load_sem.at[part])

    smalls = [
        pltpu.make_async_copy(src, dst, small_sem.at[i])
        for i, (src, dst) in enumerate((
            (w_proj_hbm, w_proj), (ln_gain_hbm, ln_gain), (w_gate_hbm, w_gate),
            (out_gain_hbm, out_gain), (w_out_hbm, w_out),
        ))
    ]
    smalls[0].start()
    for part in range(PARTS):
        load(part).start()
    for copy in smalls[1:]:
        copy.start()

    def peer(k):
        dx, dy, de = OFFSETS[k]
        px, py, pe = (x + dx) % 4, (y + dy) % 4, (e + de) % 2
        return px // 2, (px % 2) * 8 + py * 2 + pe

    beside = (((z + 1) % RING * 2 + xh, c), ((z + RING - 1) % RING * 2 + xh, c))

    barrier = pltpu.get_barrier_semaphore()

    for k in range(LAYER - 1):
        ph, pc = peer(k)
        pl.semaphore_signal(barrier, inc=1, device_id=(2 * z + ph, pc), device_id_type=MESH)

    for way in range(2):
        pl.semaphore_signal(barrier, inc=1, device_id=beside[way], device_id_type=MESH)

    wide[:, :, 128:] = jnp.zeros((BLK, 128, 128), jnp.bfloat16)
    wide[:, PAD:, :128] = jnp.zeros((BLK, PAD, 128), jnp.bfloat16)
    wide[:, BLK:PAD, :128] = jnp.zeros((BLK, PAD - BLK, 128), jnp.bfloat16)
    for copy in smalls:
        copy.wait()

    row = lax.broadcasted_iota(jnp.int32, (128, 128), 0)
    col = lax.broadcasted_iota(jnp.int32, (128, 128), 1)
    order = (col == row % HALF * 2 + row // HALF).astype(jnp.bfloat16)
    for t in range(4):
        mixed = lax.dot_general(
            order, w_proj[:, t * 128 : (t + 1) * 128], (((1,), (1,)), ((), ())), preferred_element_type=jnp.float32
        ).astype(jnp.bfloat16)
        w_wide[t // 2, t % 2 * HALF : (t % 2 + 1) * HALF, :128] = mixed[:HALF]
        w_wide[t // 2, t % 2 * HALF : (t % 2 + 1) * HALF, 128:] = mixed[HALF:]

    def project(which, msg, part):
        block = wide[pl.ds(part * SUB, SUB)].reshape(SUB * 128, 256)
        both = lax.dot_general(
            w_wide[which], block, (((1,), (1,)), ((), ())), preferred_element_type=jnp.float32
        )
        side = jax.nn.sigmoid(both[:HALF]) * both[HALF:]
        for j in range(SUB):
            stage[pl.ds(j, HALF, stride=SUB), :] = side[:, j * 128 : (j + 1) * 128]
        msg[part] = stage[pl.ds(0, HALF * SUB)].reshape(LAYER, 2 * SUB, 128).astype(jnp.bfloat16)

    def scatter(src_of, dst, send, recv):
        for k in range(LAYER - 1):
            ph, pc = peer(k)
            pltpu.make_async_remote_copy(
                src_ref=src_of(ph * 16 + pc), dst_ref=dst, send_sem=send, recv_sem=recv,
                device_id=(2 * z + ph, pc), device_id_type=MESH,
            ).start()

        pltpu.make_async_copy(src_of(me), dst, recv).start()

    def scatter_part(part):
        scatter(lambda n: b_msg.at[part, n], b_in.at[part, me], b_send.at[part], b_recv.at[part])

    def raw_copy(way):
        return pltpu.make_async_remote_copy(
            src_ref=b_msg.at[RAW], dst_ref=raw_in.at[way], send_sem=raw_send.at[way], recv_sem=raw_recv.at[way],
            device_id=beside[way], device_id_type=MESH,
        )

    def whole(ref, sem):
        pltpu.make_async_copy(ref, ref, sem).wait()

    for part in (RAW, 0, 1):
        load(part).wait()
        rows = pl.ds(part * SUB, SUB)
        values = pair[rows].astype(jnp.float32)
        average = jnp.mean(values, axis=-1, keepdims=True)
        centred = values - average
        spread = jnp.mean(centred * centred, axis=-1, keepdims=True)
        result = (centred * lax.rsqrt(spread + epsilon) * ln_gain[...].reshape(1, 1, 128)).astype(jnp.bfloat16)
        normed[rows] = result
        wide[rows, :BLK, :128] = result
        wide[rows, PAD : PAD + BLK, 128:] = result
        project(1, b_msg, part)
        if part == RAW:
            pl.semaphore_wait(barrier, LAYER + 1)
            for way in range(2):
                raw_copy(way).start()
        else:
            scatter_part(part)
    def gathered(into, h, ch):
        rows, lanes = slice(ch // 2 * SUB, (ch // 2 + 1) * SUB), slice(ch % 2 * PAD, ch % 2 * PAD + BLK)
        return jnp.concatenate([into[h * 16 + s, rows, lanes] for s in range(16)], axis=1)

    def gather_into(slot, way, part, into):
        for h in range(2):
            for ch in (2 * way, 2 * way + 1):
                b_all[slot, ch, h, part * SUB : (part + 1) * SUB, :] = gathered(into, h, ch)

    def ring_copy(step, part, way):
        block = pl.ds(2 * way, 2), slice(None), pl.ds(part * SUB, SUB)
        return pltpu.make_async_remote_copy(
            src_ref=b_all.at[(step, *block)], dst_ref=b_all.at[(step + 1, *block)],
            send_sem=ring_send.at[way, step, part], recv_sem=ring_recv.at[way, step, part],
            device_id=beside[way], device_id_type=MESH,
        )

    a_all[:, :, BLK:, :] = jnp.zeros((4, 2, PAD - BLK, K), jnp.bfloat16)
    for part in range(RAW):
        whole(b_in.at[part], b_recv.at[part])
        for way in range(2):
            gather_into(0, way, part, b_in.at[part])
            ring_copy(0, part, way).start()
    for way in range(2):
        raw_copy(way).wait_recv()
        scatter(lambda n: raw_in.at[way, n], raw_all.at[way, me], rest_send.at[way], rest_recv.at[way])

    def sent(step):
        return range(PARTS if 0 < step < RING - 2 else RAW)

    def forward(step):
        for part in sent(step - 1):
            for way in range(2):
                ring_copy(step - 1, part, way).wait_recv()
                if part in sent(step):
                    ring_copy(step, part, way).start()

    def multiply(step, way, part=None):
        count, begin = (BLK, 0) if part is None else (SUB, part * SUB)
        rows = slice(begin, begin + count)
        one, two = [
            lax.dot_general(
                b_all[step, ch, :, rows, :].reshape(2 * count, K), a_all[ch].reshape(2 * PAD, K),
                (((1,), (1,)), ((), ())), preferred_element_type=jnp.float32,
            )
            for ch in (2 * way, 2 * way + 1)
        ]
        low = lax.broadcasted_iota(jnp.int32, (2 * count, 128), 1) < PAD
        first = jnp.where(low, one, pltpu.roll(two, PAD, 1)).astype(jnp.bfloat16)
        second = jnp.where(low, pltpu.roll(one, PAD, 1), two).astype(jnp.bfloat16)
        zb = (z + RING - step if way == 0 else z + step) % RING
        for ih, value in ((0, first), (1, second)):
            for je in range(2):
                p_msg[step, way, je, ih, rows, :] = value[je * count : (je + 1) * count]
                src = p_msg.at[step, way, je, ih, pl.ds(begin, count)]
                dst = p_in.at[me + LAYER * way, pl.ds(begin, count)]
                recv = p_recv.at[PARTS + way if part is None else part]
                here = jnp.logical_and(ih == xh, 2 * zb + je == c)

                @pl.when(here)
                def _():
                    pltpu.make_async_copy(src, dst, recv).start()

                @pl.when(jnp.logical_not(here))
                def _():
                    pltpu.make_async_remote_copy(
                        src_ref=src, dst_ref=dst, send_sem=p_send, recv_sem=recv,
                        device_id=(2 * z + ih, 2 * zb + je), device_id_type=MESH,
                    ).start()

    def multiply_both(*steps):
        for step in steps:
            for way in range(2):
                multiply(step, way)

    forward(1)
    scatter_part(RAW)
    for part in range(PARTS):
        project(0, a_msg, part)
    scatter(lambda n: a_msg.at[:, n], a_in.at[:, me], a_send, a_recv)
    for way in range(2):
        whole(raw_all.at[way], rest_recv.at[way])
        gather_into(1, way, RAW, raw_all.at[way])
        ring_copy(1, RAW, way).start()
    forward(2)
    for way in range(2):
        gather_into(RING - 1, 1 - way, RAW, raw_all.at[way])
    whole(b_in.at[RAW], b_recv.at[RAW])
    for way in range(2):
        gather_into(0, way, RAW, b_in.at[RAW])

    folded = lax.dot_general(order, w_out[...], (((1,), (0,)), ((), ())), preferred_element_type=jnp.float32)
    w_fold[...] = folded.astype(jnp.bfloat16)
    pairs = lax.broadcasted_iota(jnp.int32, (HALF, 128), 0)
    lanes = lax.broadcasted_iota(jnp.int32, (HALF, 128), 1)
    under = lanes < PAD
    picked = [
        jnp.sum(jnp.where(lanes == 2 * pairs + i, out_gain[...], 0.0), axis=1, keepdims=True) for i in range(2)
    ]
    gain[...] = jnp.where(under, picked[0], picked[1])

    @pl.loop(0, PARTS)
    def _(part):
        rows = pl.ds(part * SUB, SUB)
        gate = jnp.dot(normed[rows].reshape(SUB * BLK, 128), w_gate[...], preferred_element_type=jnp.float32)
        gating[rows] = jax.nn.sigmoid(gate).reshape(SUB, BLK, 128)

    forward(3)
    whole(a_in, a_recv)
    for part in range(PARTS):
        for ch in range(4):
            for h in range(2):
                a_all[ch, h, part * SUB : (part + 1) * SUB, :] = gathered(a_in.at[part], h, ch)
    multiply_both(0, 1)
    forward(4)
    multiply_both(2, 3)
    forward(5)
    multiply_both(4, 5)
    forward(6)
    multiply_both(6)
    for way in range(2):
        multiply(RING - 1, way, RAW)
    for part in sent(RING - 2):
        for way in range(2):
            ring_copy(RING - 2, part, way).wait_recv()
            multiply(RING - 1, way, part)

    distance = (z + RING - c // 2) % RING
    for way in range(2):
        last = distance == (RING - 1 if way == 0 else 1)

        @pl.when(jnp.logical_not(last))
        def _():
            whole(p_in.at[pl.ds(LAYER * way, LAYER)], p_recv.at[PARTS + way])

    for part in (RAW, *sent(RING - 2)):
        rows = pl.ds(part * SUB, SUB)
        for way in range(2):
            last = distance == (RING - 1 if way == 0 else 1)

            @pl.when(last)
            def _():
                whole(p_in.at[pl.ds(LAYER * way, LAYER), rows], p_recv.at[part])

        slots = [n // 2 + LAYER * (n % 2) for n in range(HALF)]
        total = jnp.zeros((SUB, 128), jnp.float32)
        for s in slots:
            total = total + p_in[s, rows, :].astype(jnp.float32)
        average = (total + pltpu.roll(total, PAD, 1)) * (1.0 / 128)
        total = jnp.zeros((SUB, 128), jnp.float32)
        for s in slots:
            centred = p_in[s, rows, :].astype(jnp.float32) - average
            total = total + centred * centred
        spread = (total + pltpu.roll(total, PAD, 1)) * (1.0 / 128)
        factor = lax.rsqrt(spread + epsilon)
        for n, s in enumerate(slots):
            centred = p_in[s, rows, :].astype(jnp.float32) - average
            stage[n * SUB : (n + 1) * SUB, :] = centred * factor * gain[n : n + 1, :]

        for n in range(2):
            blocks = []
            for i in range(4):
                one = stage[pl.ds(8 * n + 2 * i, HALF, stride=SUB), :]
                two = stage[pl.ds(8 * n + 2 * i + 1, HALF, stride=SUB), :]
                even = jnp.where(under, one, pltpu.roll(two, PAD, 1))
                odd = jnp.where(under, pltpu.roll(one, PAD, 1), two)
                blocks.append(jnp.concatenate([even, odd], axis=0).astype(jnp.bfloat16))
            both = jnp.concatenate(blocks, axis=1)
            result = lax.dot_general(
                both, w_fold[...], (((0,), (0,)), ((), ())), preferred_element_type=jnp.float32
            )
            for j in range(8):
                turned[pl.ds(part * SUB + 8 * n + j, BLK, stride=BLK), :] = result[j * PAD : j * PAD + BLK]

    @pl.loop(0, PARTS)
    def _(part):
        rows = pl.ds(part * SUB, SUB)
        result = turned[pl.ds(part * SUB * BLK, SUB * BLK), :].reshape(SUB, BLK, 128)
        out[rows] = (gating[rows] * result).astype(jnp.bfloat16)

    for part in range(PARTS):
        whole(b_msg.at[part, pl.ds(0, LAYER - 1)], b_send.at[part])
    whole(a_msg.at[:, pl.ds(0, LAYER - 1)], a_send)
    whole(p_in.at[pl.ds(0, 2 * (LAYER - 1))], p_send)
    for way in range(2):
        raw_copy(way).wait_send()
        whole(raw_in.at[way, pl.ds(0, LAYER - 1)], rest_send.at[way])
        for step in range(RING - 1):
            for part in sent(step):
                ring_copy(step, part, way).wait_send()


def per_device(pair, ln_gain, w_proj, w_gate, out_gain, w_out):
    bf16, f32 = jnp.bfloat16, jnp.float32
    vmem = pl.BlockSpec(memory_space=pltpu.VMEM)
    dma = pltpu.SemaphoreType.DMA
    parts = (PARTS, LAYER, 2 * SUB, 128)
    return pl.pallas_call(
        kernel,
        out_shape=jax.ShapeDtypeStruct(pair.shape, bf16),
        in_specs=[pl.BlockSpec(memory_space=pl.ANY)] * 6,
        out_specs=vmem,
        scratch_shapes=[
            pltpu.VMEM((BLK, BLK, 128), bf16),
            pltpu.VMEM((1, 128), f32),
            pltpu.VMEM((128, 512), bf16),
            pltpu.VMEM((128, 128), bf16),
            pltpu.VMEM((1, 128), f32),
            pltpu.VMEM((128, 128), bf16),
            pltpu.VMEM((BLK, BLK, 128), bf16),
            pltpu.VMEM((BLK, 128, 256), bf16),
            pltpu.VMEM((HALF * BLK, 128), f32),
            pltpu.VMEM((BLK, BLK, 128), f32),
            pltpu.VMEM((2, 128, 256), bf16),
            pltpu.VMEM((128, 128), bf16),
            pltpu.VMEM((HALF, 128), f32),
            pltpu.VMEM(parts, bf16),
            pltpu.VMEM(parts, bf16),
            pltpu.VMEM(parts, bf16),
            pltpu.VMEM(parts, bf16),
            pltpu.VMEM((2, *parts[1:]), bf16),
            pltpu.VMEM((2, *parts[1:]), bf16),
            pltpu.VMEM((4, 2, PAD, K), bf16),
            pltpu.VMEM((RING, 4, 2, BLK, K), bf16),
            pltpu.VMEM((RING, 2, 2, 2, BLK, 128), bf16),
            pltpu.VMEM((2 * LAYER, BLK, 128), bf16),
            pltpu.VMEM((BLK * BLK, 128), f32),
            dma((PARTS,)), dma((5,)),
            dma((PARTS,)), dma((PARTS,)), dma, dma,
            dma((2,)), dma((2,)), dma((2,)), dma((2,)),
            dma, dma((PARTS + 2,)),
            dma((2, RING - 1, PARTS)), dma((2, RING - 1, PARTS)),
        ],
        compiler_params=pltpu.CompilerParams(
            collective_id=0, has_side_effects=True, vmem_limit_bytes=56 * 2**20
        ),
        name="triangle",
    )(pair, ln_gain.reshape(1, 128), w_proj, w_gate, out_gain.reshape(1, 128), w_out)


def solution(mesh):
    in_specs = (P("row", "col", None), P(), P(), P(), P(), P())
    out_specs = P("row", "col", None)
    return jax.shard_map(per_device, mesh=mesh, in_specs=in_specs, out_specs=out_specs, check_vma=False)
```

```python
import jax
import jax.numpy as jnp
from jax import lax
from jax.experimental import pallas as pl
from jax.experimental.pallas import tpu as pltpu
from jax.sharding import PartitionSpec as P

epsilon = 1e-05
MESH = pl.DeviceIdType.MESH
BLK = 48
PAD = 64
HALF = 64
LAYER = 32
RING = 8
K = 768
SUB = 16
PARTS = BLK // SUB
RAW = PARTS - 1


OFFSETS = [(2, 2, 0), (2, 2, 1), (2, 3, 0), (2, 3, 1), (3, 2, 0), (3, 2, 1), (2, 1, 0), (2, 1, 1), (1, 2, 0), (1, 2, 1), (2, 0, 0), (2, 0, 1), (0, 2, 0), (0, 2, 1), (3, 1, 0), (3, 1, 1), (1, 3, 0), (1, 3, 1), (3, 3, 0), (3, 3, 1), (1, 1, 0), (1, 1, 1), (3, 0, 0), (3, 0, 1), (0, 3, 0), (0, 3, 1), (1, 0, 0), (1, 0, 1), (0, 1, 0), (0, 1, 1), (0, 0, 1)]


def kernel(
    pair_hbm, ln_gain_hbm, w_proj_hbm, w_gate_hbm, out_gain_hbm, w_out_hbm, out,
    pair, ln_gain, w_proj, w_gate, out_gain, w_out, normed, wide, stage, gating, w_wide, w_fold, gain,
    b_msg, a_msg, b_in, a_in, raw_in, raw_all, a_all, b_all, p_msg, p_in, turned,
    load_sem, small_sem, b_send, b_recv, a_send, a_recv, raw_send, raw_recv, rest_send, rest_recv, p_send, p_recv, ring_send, ring_recv,
):
    r, c = lax.axis_index("row"), lax.axis_index("col")
    z, xh = r // 2, r % 2
    x, y, e = xh * 2 + c // 8, (c // 2) % 4, c % 2
    me = xh * 16 + c

    def load(part):
        rows = pl.ds(part * SUB, SUB)
        return pltpu.make_async_copy(pair_hbm.at[rows], pair.at[rows], load_sem.at[part])

    smalls = [
        pltpu.make_async_copy(src, dst, small_sem.at[i])
        for i, (src, dst) in enumerate((
            (w_proj_hbm, w_proj), (ln_gain_hbm, ln_gain), (w_gate_hbm, w_gate),
            (out_gain_hbm, out_gain), (w_out_hbm, w_out),
        ))
    ]
    smalls[0].start()
    for part in range(PARTS):
        load(part).start()
    for copy in smalls[1:]:
        copy.start()

    def peer(k):
        dx, dy, de = OFFSETS[k]
        px, py, pe = (x + dx) % 4, (y + dy) % 4, (e + de) % 2
        return px // 2, (px % 2) * 8 + py * 2 + pe

    beside = (((z + 1) % RING * 2 + xh, c), ((z + RING - 1) % RING * 2 + xh, c))

    barrier = pltpu.get_barrier_semaphore()

    for k in range(LAYER - 1):
        ph, pc = peer(k)
        pl.semaphore_signal(barrier, inc=1, device_id=(2 * z + ph, pc), device_id_type=MESH)

    for way in range(2):
        pl.semaphore_signal(barrier, inc=1, device_id=beside[way], device_id_type=MESH)

    wide[:, :, 128:] = jnp.zeros((BLK, 128, 128), jnp.bfloat16)
    wide[:, PAD:, :128] = jnp.zeros((BLK, PAD, 128), jnp.bfloat16)
    wide[:, BLK:PAD, :128] = jnp.zeros((BLK, PAD - BLK, 128), jnp.bfloat16)
    for copy in smalls:
        copy.wait()

    row = lax.broadcasted_iota(jnp.int32, (128, 128), 0)
    col = lax.broadcasted_iota(jnp.int32, (128, 128), 1)
    order = (col == row % HALF * 2 + row // HALF).astype(jnp.bfloat16)
    for t in range(4):
        mixed = lax.dot_general(
            order, w_proj[:, t * 128 : (t + 1) * 128], (((1,), (1,)), ((), ())), preferred_element_type=jnp.float32
        ).astype(jnp.bfloat16)
        w_wide[t // 2, t % 2 * HALF : (t % 2 + 1) * HALF, :128] = mixed[:HALF]
        w_wide[t // 2, t % 2 * HALF : (t % 2 + 1) * HALF, 128:] = mixed[HALF:]

    def project(which, msg, part):
        block = wide[pl.ds(part * SUB, SUB)].reshape(SUB * 128, 256)
        both = lax.dot_general(
            w_wide[which], block, (((1,), (1,)), ((), ())), preferred_element_type=jnp.float32
        )
        side = jax.nn.sigmoid(both[:HALF]) * both[HALF:]
        for j in range(SUB):
            stage[pl.ds(j, HALF, stride=SUB), :] = side[:, j * 128 : (j + 1) * 128]
        msg[part] = stage[pl.ds(0, HALF * SUB)].reshape(LAYER, 2 * SUB, 128).astype(jnp.bfloat16)

    def scatter(src_of, dst, send, recv):
        for k in range(LAYER - 1):
            ph, pc = peer(k)
            pltpu.make_async_remote_copy(
                src_ref=src_of(ph * 16 + pc), dst_ref=dst, send_sem=send, recv_sem=recv,
                device_id=(2 * z + ph, pc), device_id_type=MESH,
            ).start()

        pltpu.make_async_copy(src_of(me), dst, recv).start()

    def scatter_part(part):
        scatter(lambda n: b_msg.at[part, n], b_in.at[part, me], b_send.at[part], b_recv.at[part])

    def raw_copy(way):
        return pltpu.make_async_remote_copy(
            src_ref=b_msg.at[RAW], dst_ref=raw_in.at[way], send_sem=raw_send.at[way], recv_sem=raw_recv.at[way],
            device_id=beside[way], device_id_type=MESH,
        )

    def whole(ref, sem):
        pltpu.make_async_copy(ref, ref, sem).wait()

    for part in (RAW, 0, 1):
        load(part).wait()
        rows = pl.ds(part * SUB, SUB)
        values = pair[rows].astype(jnp.float32)
        average = jnp.mean(values, axis=-1, keepdims=True)
        centred = values - average
        spread = jnp.mean(centred * centred, axis=-1, keepdims=True)
        result = (centred * lax.rsqrt(spread + epsilon) * ln_gain[...].reshape(1, 1, 128)).astype(jnp.bfloat16)
        normed[rows] = result
        wide[rows, :BLK, :128] = result
        wide[rows, PAD : PAD + BLK, 128:] = result
        project(1, b_msg, part)
        if part == RAW:
            pl.semaphore_wait(barrier, LAYER + 1)
            for way in range(2):
                raw_copy(way).start()
        else:
            scatter_part(part)
    def gathered(into, h, ch):
        rows, lanes = slice(ch // 2 * SUB, (ch // 2 + 1) * SUB), slice(ch % 2 * PAD, ch % 2 * PAD + BLK)
        return jnp.concatenate([into[h * 16 + s, rows, lanes] for s in range(16)], axis=1)

    def gather_into(slot, way, part, into):
        for h in range(2):
            for ch in (2 * way, 2 * way + 1):
                b_all[slot, ch, h, part * SUB : (part + 1) * SUB, :] = gathered(into, h, ch)

    def ring_copy(step, part, way):
        block = pl.ds(2 * way, 2), slice(None), pl.ds(part * SUB, SUB)
        return pltpu.make_async_remote_copy(
            src_ref=b_all.at[(step, *block)], dst_ref=b_all.at[(step + 1, *block)],
            send_sem=ring_send.at[way, step, part], recv_sem=ring_recv.at[way, step, part],
            device_id=beside[way], device_id_type=MESH,
        )

    a_all[:, :, BLK:, :] = jnp.zeros((4, 2, PAD - BLK, K), jnp.bfloat16)
    for part in range(RAW):
        whole(b_in.at[part], b_recv.at[part])
        for way in range(2):
            gather_into(0, way, part, b_in.at[part])
            ring_copy(0, part, way).start()
    for way in range(2):
        raw_copy(way).wait_recv()
        scatter(lambda n: raw_in.at[way, n], raw_all.at[way, me], rest_send.at[way], rest_recv.at[way])

    def sent(step):
        return range(PARTS if 0 < step < RING - 2 else RAW)

    def forward(step):
        for part in sent(step - 1):
            for way in range(2):
                ring_copy(step - 1, part, way).wait_recv()
                if part in sent(step):
                    ring_copy(step, part, way).start()

    def multiply(step, way, part=None):
        count, begin = (BLK, 0) if part is None else (SUB, part * SUB)
        rows = slice(begin, begin + count)
        one, two = [
            lax.dot_general(
                b_all[step, ch, :, rows, :].reshape(2 * count, K), a_all[ch].reshape(2 * PAD, K),
                (((1,), (1,)), ((), ())), preferred_element_type=jnp.float32,
            )
            for ch in (2 * way, 2 * way + 1)
        ]
        low = lax.broadcasted_iota(jnp.int32, (2 * count, 128), 1) < PAD
        first = jnp.where(low, one, pltpu.roll(two, PAD, 1)).astype(jnp.bfloat16)
        second = jnp.where(low, pltpu.roll(one, PAD, 1), two).astype(jnp.bfloat16)
        zb = (z + RING - step if way == 0 else z + step) % RING
        for ih, value in ((0, first), (1, second)):
            for je in range(2):
                p_msg[step, way, je, ih, rows, :] = value[je * count : (je + 1) * count]
                src = p_msg.at[step, way, je, ih, pl.ds(begin, count)]
                dst = p_in.at[me + LAYER * way, pl.ds(begin, count)]
                recv = p_recv.at[PARTS + way if part is None else part]
                here = jnp.logical_and(ih == xh, 2 * zb + je == c)

                @pl.when(here)
                def _():
                    pltpu.make_async_copy(src, dst, recv).start()

                @pl.when(jnp.logical_not(here))
                def _():
                    pltpu.make_async_remote_copy(
                        src_ref=src, dst_ref=dst, send_sem=p_send, recv_sem=recv,
                        device_id=(2 * z + ih, 2 * zb + je), device_id_type=MESH,
                    ).start()

    def multiply_both(*steps):
        for step in steps:
            for way in range(2):
                multiply(step, way)

    forward(1)
    scatter_part(RAW)
    for part in range(PARTS):
        project(0, a_msg, part)
    scatter(lambda n: a_msg.at[:, n], a_in.at[:, me], a_send, a_recv)
    for way in range(2):
        whole(raw_all.at[way], rest_recv.at[way])
        gather_into(1, way, RAW, raw_all.at[way])
        ring_copy(1, RAW, way).start()
    forward(2)
    for way in range(2):
        gather_into(RING - 1, 1 - way, RAW, raw_all.at[way])
    whole(b_in.at[RAW], b_recv.at[RAW])
    for way in range(2):
        gather_into(0, way, RAW, b_in.at[RAW])

    forward(3)
    whole(a_in, a_recv)
    for part in range(PARTS):
        for ch in range(4):
            for h in range(2):
                a_all[ch, h, part * SUB : (part + 1) * SUB, :] = gathered(a_in.at[part], h, ch)
    multiply_both(0, 1)
    forward(4)
    multiply_both(2, 3)
    forward(5)
    multiply_both(4, 5)

    folded = lax.dot_general(order, w_out[...], (((1,), (0,)), ((), ())), preferred_element_type=jnp.float32)
    w_fold[...] = folded.astype(jnp.bfloat16)
    pairs = lax.broadcasted_iota(jnp.int32, (HALF, 128), 0)
    lanes = lax.broadcasted_iota(jnp.int32, (HALF, 128), 1)
    under = lanes < PAD
    picked = [
        jnp.sum(jnp.where(lanes == 2 * pairs + i, out_gain[...], 0.0), axis=1, keepdims=True) for i in range(2)
    ]
    gain[...] = jnp.where(under, picked[0], picked[1])

    @pl.loop(0, PARTS)
    def _(part):
        rows = pl.ds(part * SUB, SUB)
        gate = jnp.dot(normed[rows].reshape(SUB * BLK, 128), w_gate[...], preferred_element_type=jnp.float32)
        gating[rows] = jax.nn.sigmoid(gate).reshape(SUB, BLK, 128)

    forward(6)
    multiply_both(6)
    for way in range(2):
        multiply(RING - 1, way, RAW)
    for part in sent(RING - 2):
        for way in range(2):
            ring_copy(RING - 2, part, way).wait_recv()
            multiply(RING - 1, way, part)

    distance = (z + RING - c // 2) % RING
    for way in range(2):
        last = distance == (RING - 1 if way == 0 else 1)

        @pl.when(jnp.logical_not(last))
        def _():
            whole(p_in.at[pl.ds(LAYER * way, LAYER)], p_recv.at[PARTS + way])

    for part in (RAW, *sent(RING - 2)):
        rows = pl.ds(part * SUB, SUB)
        for way in range(2):
            last = distance == (RING - 1 if way == 0 else 1)

            @pl.when(last)
            def _():
                whole(p_in.at[pl.ds(LAYER * way, LAYER), rows], p_recv.at[part])

        slots = [n // 2 + LAYER * (n % 2) for n in range(HALF)]
        total = jnp.zeros((SUB, 128), jnp.float32)
        for s in slots:
            total = total + p_in[s, rows, :].astype(jnp.float32)
        average = (total + pltpu.roll(total, PAD, 1)) * (1.0 / 128)
        total = jnp.zeros((SUB, 128), jnp.float32)
        for s in slots:
            centred = p_in[s, rows, :].astype(jnp.float32) - average
            total = total + centred * centred
        spread = (total + pltpu.roll(total, PAD, 1)) * (1.0 / 128)
        factor = lax.rsqrt(spread + epsilon)
        for n, s in enumerate(slots):
            centred = p_in[s, rows, :].astype(jnp.float32) - average
            stage[n * SUB : (n + 1) * SUB, :] = centred * factor * gain[n : n + 1, :]

        for n in range(2):
            blocks = []
            for i in range(4):
                one = stage[pl.ds(8 * n + 2 * i, HALF, stride=SUB), :]
                two = stage[pl.ds(8 * n + 2 * i + 1, HALF, stride=SUB), :]
                even = jnp.where(under, one, pltpu.roll(two, PAD, 1))
                odd = jnp.where(under, pltpu.roll(one, PAD, 1), two)
                blocks.append(jnp.concatenate([even, odd], axis=0).astype(jnp.bfloat16))
            both = jnp.concatenate(blocks, axis=1)
            result = lax.dot_general(
                both, w_fold[...], (((0,), (0,)), ((), ())), preferred_element_type=jnp.float32
            )
            for j in range(8):
                turned[pl.ds(part * SUB + 8 * n + j, BLK, stride=BLK), :] = result[j * PAD : j * PAD + BLK]

    @pl.loop(0, PARTS)
    def _(part):
        rows = pl.ds(part * SUB, SUB)
        result = turned[pl.ds(part * SUB * BLK, SUB * BLK), :].reshape(SUB, BLK, 128)
        out[rows] = (gating[rows] * result).astype(jnp.bfloat16)

    for part in range(PARTS):
        whole(b_msg.at[part, pl.ds(0, LAYER - 1)], b_send.at[part])
    whole(a_msg.at[:, pl.ds(0, LAYER - 1)], a_send)
    whole(p_in.at[pl.ds(0, 2 * (LAYER - 1))], p_send)
    for way in range(2):
        raw_copy(way).wait_send()
        whole(raw_in.at[way, pl.ds(0, LAYER - 1)], rest_send.at[way])
        for step in range(RING - 1):
            for part in sent(step):
                ring_copy(step, part, way).wait_send()


def per_device(pair, ln_gain, w_proj, w_gate, out_gain, w_out):
    bf16, f32 = jnp.bfloat16, jnp.float32
    vmem = pl.BlockSpec(memory_space=pltpu.VMEM)
    dma = pltpu.SemaphoreType.DMA
    parts = (PARTS, LAYER, 2 * SUB, 128)
    return pl.pallas_call(
        kernel,
        out_shape=jax.ShapeDtypeStruct(pair.shape, bf16),
        in_specs=[pl.BlockSpec(memory_space=pl.ANY)] * 6,
        out_specs=vmem,
        scratch_shapes=[
            pltpu.VMEM((BLK, BLK, 128), bf16),
            pltpu.VMEM((1, 128), f32),
            pltpu.VMEM((128, 512), bf16),
            pltpu.VMEM((128, 128), bf16),
            pltpu.VMEM((1, 128), f32),
            pltpu.VMEM((128, 128), bf16),
            pltpu.VMEM((BLK, BLK, 128), bf16),
            pltpu.VMEM((BLK, 128, 256), bf16),
            pltpu.VMEM((HALF * BLK, 128), f32),
            pltpu.VMEM((BLK, BLK, 128), f32),
            pltpu.VMEM((2, 128, 256), bf16),
            pltpu.VMEM((128, 128), bf16),
            pltpu.VMEM((HALF, 128), f32),
            pltpu.VMEM(parts, bf16),
            pltpu.VMEM(parts, bf16),
            pltpu.VMEM(parts, bf16),
            pltpu.VMEM(parts, bf16),
            pltpu.VMEM((2, *parts[1:]), bf16),
            pltpu.VMEM((2, *parts[1:]), bf16),
            pltpu.VMEM((4, 2, PAD, K), bf16),
            pltpu.VMEM((RING, 4, 2, BLK, K), bf16),
            pltpu.VMEM((RING, 2, 2, 2, BLK, 128), bf16),
            pltpu.VMEM((2 * LAYER, BLK, 128), bf16),
            pltpu.VMEM((BLK * BLK, 128), f32),
            dma((PARTS,)), dma((5,)),
            dma((PARTS,)), dma((PARTS,)), dma, dma,
            dma((2,)), dma((2,)), dma((2,)), dma((2,)),
            dma, dma((PARTS + 2,)),
            dma((2, RING - 1, PARTS)), dma((2, RING - 1, PARTS)),
        ],
        compiler_params=pltpu.CompilerParams(
            collective_id=0, has_side_effects=True, vmem_limit_bytes=56 * 2**20
        ),
        name="triangle",
    )(pair, ln_gain.reshape(1, 128), w_proj, w_gate, out_gain.reshape(1, 128), w_out)


def solution(mesh):
    in_specs = (P("row", "col", None), P(), P(), P(), P(), P())
    out_specs = P("row", "col", None)
    return jax.shard_map(per_device, mesh=mesh, in_specs=in_specs, out_specs=out_specs, check_vma=False)
```
